32 devices in a mesh: dp: 4 (over z), row: 2 (over y), col: 4 (over x, core).
Axes of the slice: x: 2, y: 2, z: 4, core: 2. Of those that a mesh axis runs over, the one named last changes fastest.
Arguments:
- tokens_in: bfloat16 [16384, 1536], P(('dp', 'col'), 'row'), may hold values from -6 to 6
- norm1_gain: float32 [1536], P('row'), may hold values from 0.1 to 1.9
- w_query: bfloat16 [1536, 1536], P('row', 'col'), may hold values from -0.15625 to 0.15625
- w_keyval: bfloat16 [1536, 256], P('row'), may hold values from -0.15625 to 0.15625
- w_attn_out: bfloat16 [1536, 1536], P('col', 'row'), may hold values from -1.25 to 1.25
- norm2_gain: float32 [1536], P('row'), may hold values from 0.1 to 1.9
- w_gate: bfloat16 [1536, 4608], P('row', 'col'), may hold values from -0.15625 to 0.15625
- w_up: bfloat16 [1536, 4608], P('row', 'col'), may hold values from -0.15625 to 0.15625
- w_down: bfloat16 [4608, 1536], P('col', 'row'), may hold values from -0.1875 to 0.1875
- segment_ids: int32 [8, 2048], P(('dp', 'row')), may hold values from 0 to 5, never falling along the last dimension, each value on 1 to 800 neighbouring positions
- out_cotangent: bfloat16 [16384, 1536], P(('dp', 'col'), 'row'), may hold values from -6 to 6
Outputs:
- output: float32 [16384, 1536], P(('dp', 'col'), 'row')
- input_grad: float32 [16384, 1536], P(('dp', 'col'), 'row')
- w_query_grad: float32 [1536, 1536], P('row', 'col')
- w_keyval_grad: float32 [1536, 256], P('row')
- w_attn_out_grad: float32 [1536, 1536], P('col', 'row')
- w_gate_grad: float32 [1536, 4608], P('row', 'col')
- w_up_grad: float32 [1536, 4608], P('row', 'col')
- w_down_grad: float32 [4608, 1536], P('col', 'row')
- norm1_gain_grad: float32 [1536], P('row')
- norm2_gain_grad: float32 [1536], P('row')
The draws below stay inside these ranges and needn't reach their ends.
Inputs may be any that keep to these rules, and one draw needn't show every extreme that they name: `segment_ids`: document numbers never fall along a sequence; a run of equal numbers has at most 800 tokens.
All inputs are finite; a program needn't handle non-finite values.
Results may differ from the reference program's by a relative error of at most 0.018.
Values may be sent and summed in bfloat16 or wider, within the bound.
No kernel may reach another device: no remote copies, remote signals or barrier semaphores. Data moves between devices by JAX's collectives and lax.ppermute only.
A program may use at most 256 MiB of HBM per device.

```python
import math
import jax
import jax.numpy as jnp
import numpy as np
from jax import lax

D = 1536
HEADS = 12
HD = 128
FF = 4608
WINDOW = 1024
SEQ = 2048
SEGS = 6
DOC_MOST = 800
QD = 1536
NSEQ = 8
TOKENS = 16384
N_COL = 4


def steps_of(key, extent, split, low, top_value):
    level, own = 1.0, jax.random.fold_in(key, 6)
    for axis_at, parts in split:
        draws = jnp.exp(jax.random.uniform(jax.random.fold_in(own, axis_at), (parts,), jnp.float32, low / len(split), top_value / len(split)))
        level = level * jnp.repeat(draws, extent[axis_at] // parts).reshape([-1 if axis == axis_at else 1 for axis in range(len(extent))])
    return level


def split_up(amount, total, bound, skew):
    weights = [(1 << 20) // math.isqrt(rank ** skew) + 1 for rank in range(2, amount + 1)]
    surplus, given = total - bound - (amount - 1), [1] * (amount - 1)
    while surplus > 0:
        movable = [i for i in range(amount - 1) if given[i] < bound]
        whole, left = sum([weights[i] for i in movable]), surplus
        for i in movable:
            extra = min(bound - given[i], max(1, left * weights[i] // whole), surplus)
            given[i] = given[i] + extra
            surplus = surplus - extra
    return np.array([bound] + given)


def uneven(stream_key, number_of, total, bound, skew):
    if number_of == 2:
        one = jax.random.randint(stream_key, (), max(1, total - bound), min(bound, total - 1) + 1)
        return jnp.stack([one, total - one])
    tallies = jnp.asarray(split_up(number_of, total, bound, skew), jnp.int32)
    pairs = (number_of - 1) // 2
    source_of, sink = tallies[1:1 + 2 * pairs:2], tallies[2:2 + 2 * pairs:2]
    slack = jnp.minimum(source_of - 1, bound - sink)
    passed = jax.random.randint(jax.random.fold_in(stream_key, 1), (pairs,), 0, 1 << 20) % (slack + 1)
    tallies = tallies.at[1:1 + 2 * pairs:2].set(source_of - passed).at[2:2 + 2 * pairs:2].set(sink + passed)
    return tallies[jax.random.permutation(jax.random.fold_in(stream_key, 2), number_of)]


def centred(rng, dims, width, most, cuts=(), held_as=jnp.bfloat16):
    values = width * jax.random.normal(rng, dims, jnp.float32)
    if cuts:
        values = values * steps_of(rng, dims, cuts, -0.22, 0.18)
    return jnp.clip(values, -most, most).astype(held_as)


def setup_inputs(seed: int = 0) -> dict:
    seeds = jax.random.split(jax.random.key(seed), 12)
    return {
        "tokens_in": centred(seeds[0], (TOKENS, D), 1.0, 6.0, ((0, 16), (1, 2))),
        "norm1_gain": jnp.clip(1.0 + 0.18 * jax.random.normal(seeds[1], (D,), jnp.float32), 0.1, 1.9),
        "w_query": centred(seeds[2], (D, QD), D ** -0.5, 0.15625, ((0, 2), (1, 4))),
        "w_keyval": centred(seeds[3], (D, 2 * HD), D ** -0.5, 0.15625, ((0, 2),)),
        "w_attn_out": centred(seeds[4], (QD, D), (QD // 64) ** -0.5, 1.25, ((0, 4), (1, 2))),
        "norm2_gain": jnp.clip(1.0 + 0.18 * jax.random.normal(seeds[5], (D,), jnp.float32), 0.1, 1.9),
        "w_gate": centred(seeds[6], (D, FF), D ** -0.5, 0.15625, ((0, 2), (1, 4))),
        "w_up": centred(seeds[7], (D, FF), D ** -0.5, 0.15625, ((0, 2), (1, 4))),
        "w_down": centred(seeds[8], (FF, D), (FF // 4) ** -0.5, 0.1875, ((0, 4), (1, 2))),
        "segment_ids": jax.vmap(lambda own: jnp.searchsorted(jnp.cumsum(uneven(own, SEGS, SEQ, DOC_MOST, 0)), jnp.arange(SEQ), side="right"))(jax.random.split(seeds[9], NSEQ)).reshape((NSEQ, SEQ)).astype(jnp.int32),
        "out_cotangent": centred(seeds[10], (TOKENS, D), 1.0, 6.0, ((0, 16), (1, 2))),
    }


EPSILON = 1e-06
NEGATIVE = -1e+30

@jax.custom_vjp
def low(v):
    return lax.optimization_barrier(v.astype(jnp.bfloat16)).astype(jnp.float32)

@jax.custom_vjp
def low_back(v):
    return v

def low_keep(v):
    return (low(v), None)

def low_pass(kept, grad):
    return (grad,)

def back_keep(v):
    return (v, None)

def back_low(kept, grad):
    return (low(grad),)
low.defvjp(low_keep, low_pass)
low_back.defvjp(back_keep, back_low)

def matmul(left, right):
    return jnp.dot(left, right, precision=lax.Precision.HIGHEST)

def rms_normed(values, gain):
    inverse = lax.rsqrt(lax.optimization_barrier(jnp.mean(values * values, axis=1, keepdims=True)) + EPSILON)
    return low(values * inverse * gain)

def attend(inputs):
    queries, keyval, segment_row = inputs
    positions = jnp.arange(SEQ)
    distance = positions[:, None] - positions[None, :]
    allowed = (segment_row[:, None] == segment_row[None, :]) & (distance >= 0) & (distance < WINDOW)
    grouped = queries.reshape(SEQ, N_COL, HEADS // N_COL, HD)
    scale = 1.0 / math.sqrt(HD)
    pieces = []
    for group_index in range(N_COL):
        shared = low_back(keyval)
        key_rows = shared[:, :HD]
        value_rows = shared[:, HD:]
        scores = jnp.einsum('qhd,kd->hqk', grouped[:, group_index], key_rows, precision=lax.Precision.HIGHEST) * scale
        scores = low_back(scores)
        scores = jnp.where(allowed[None], scores, NEGATIVE)
        attn_probs = low(jax.nn.softmax(scores, axis=-1))
        pieces.append(jnp.einsum('hqk,kd->qhd', attn_probs, value_rows, precision=lax.Precision.HIGHEST))
    return jnp.concatenate(pieces, axis=1).reshape(SEQ, HEADS * HD)

def forward(tokens, gain_one, w_query, w_keyval, w_attn_out, gain_two, w_gate, w_up, w_down, segment_ids):
    normed_one = rms_normed(tokens, gain_one)
    queries = low_back(low(matmul(normed_one, w_query)))
    keyval = low(matmul(normed_one, w_keyval))
    context = lax.map(jax.checkpoint(attend), (queries.reshape(-1, SEQ, HEADS, HD), keyval.reshape(-1, SEQ, 2 * HD), segment_ids))
    context = low_back(low(context.reshape(tokens.shape[0], HEADS * HD)))
    middle = tokens + low_back(matmul(context, w_attn_out))
    normed_two = rms_normed(middle, gain_two)
    gate = low_back(matmul(normed_two, w_gate))
    upward = low_back(matmul(normed_two, w_up))
    hidden = low(jax.nn.gelu(gate) * upward)
    return middle + low_back(matmul(hidden, w_down))

def reference(tokens_in, norm1_gain, w_query, w_keyval, w_attn_out, norm2_gain, w_gate, w_up, w_down, segment_ids, out_cotangent):
    floats = [array_in.astype(jnp.float32) for array_in in (tokens_in, norm1_gain, w_query, w_keyval, w_attn_out, norm2_gain, w_gate, w_up, w_down)]

    def closed(*params):
        return forward(*params, segment_ids)
    output, pullback = jax.vjp(closed, *floats)
    grads = pullback(out_cotangent.astype(jnp.float32))
    return (output, grads[0], grads[2], grads[3], grads[4], grads[6], grads[7], grads[8], grads[1], grads[5])
```

```python
import functools
import math

import jax
import jax.numpy as jnp
from jax import lax
from jax.experimental import pallas as pl
from jax.experimental.pallas import tpu as pltpu
from jax.sharding import PartitionSpec as P

D = 1536
HD = 128
WINDOW = 1024
EPSILON = 1e-06
NEGATIVE = -1e30
BF16 = jnp.bfloat16
F32 = jnp.float32
VMEM_BYTES = 56 * 1024 * 1024


def after(value, *earlier):
    return lax.optimization_barrier((value, *earlier))[0]


def swap_row(value):
    return lax.ppermute(value, "row", [(0, 1), (1, 0)])


def swap_core(value):
    return lax.ppermute(value, "col", [(0, 1), (1, 0), (2, 3), (3, 2)])


def swap_far(value):
    return lax.ppermute(value, "col", [(0, 2), (2, 0), (1, 3), (3, 1)])


def dot(left, right, out=F32):
    return jnp.dot(left, right, preferred_element_type=F32).astype(out)


def dot_t(left, right, out=F32):
    return lax.dot_general(
        left, right, (((1,), (1,)), ((), ())), preferred_element_type=F32
    ).astype(out)


def t_dot(left, right, out=F32):
    return lax.dot_general(
        left, right, (((0,), (0,)), ((), ())), preferred_element_type=F32
    ).astype(out)


def total_over_dp(part):
    count = lax.axis_size("dp")
    if count != 4:
        return lax.psum(part, "dp").astype(F32)
    place = lax.axis_index("dp")
    inward = lax.ppermute(part, "dp", [(0, 1), (3, 2)])
    pair = part + inward
    across = lax.ppermute(pair, "dp", [(1, 2), (2, 1)])
    both = pair + across
    back = lax.ppermute(both, "dp", [(1, 0), (2, 3)])
    outer = (place == 0) | (place == 3)
    return jnp.where(outer, back, both).astype(F32)


def gather_col(block):
    far = swap_far(block)
    near = swap_core(block)
    diagonal = swap_core(far)
    return (block, near, far, diagonal)


def scatter_col(own, near, far, diagonal):
    near_in = swap_core(near)
    diagonal_in = swap_core(diagonal)
    for_far = (far.astype(F32) + diagonal_in.astype(F32)).astype(BF16)
    far_in = swap_far(for_far)
    return own.astype(F32) + near_in.astype(F32) + far_in.astype(F32)


def block_bias(first_query, first_key, rows, cols, query_segs, key_segs):
    query_pos = first_query + lax.broadcasted_iota(jnp.int32, (rows, cols), 0)
    key_pos = first_key + lax.broadcasted_iota(jnp.int32, (rows, cols), 1)
    distance = query_pos - key_pos
    allowed = (query_segs == key_segs) & (distance >= 0) & (distance < WINDOW)
    return jnp.where(allowed, 0.0, NEGATIVE)


def first_block(first_query, query_segs, key_segs, tile_k):
    earlier = jnp.sum((key_segs < query_segs[0:1, 0:1]).astype(jnp.int32))
    return lax.div(jnp.maximum(earlier, first_query - (WINDOW - 1)), tile_k)


def attend_forward_kernel(start, q, kv, seg_q, seg_k, ctx, lse, m_s, l_s, acc_s, *, tq, tk, heads):
    first_query = start[0] + pl.program_id(0) * tq
    query_segs = seg_q[...]
    low_block = first_block(first_query, query_segs, seg_k[...], tk)
    high_block = lax.div(first_query + tq - 1, tk)
    scale = 1.0 / math.sqrt(HD)

    def step(block, first):
        first_key = pl.multiple_of(block * tk, tk)
        keys = kv[pl.ds(first_key, tk), :HD]
        values = kv[pl.ds(first_key, tk), HD:]
        bias = block_bias(first_query, first_key, tq, tk, query_segs, seg_k[:, pl.ds(first_key, tk)])
        for h in range(heads):
            cols = slice(h * HD, (h + 1) * HD)
            scores = dot_t(q[:, cols], keys) * scale + bias
            top = jnp.max(scores, axis=1, keepdims=True)
            if first:
                new = jnp.broadcast_to(top, (tq, HD))
                exps = jnp.exp(scores - top)
                l_s[:, cols] = jnp.broadcast_to(jnp.sum(exps, axis=1, keepdims=True), (tq, HD))
                acc_s[:, cols] = dot(exps.astype(BF16), values)
                m_s[:, cols] = new
            else:
                old = m_s[:, cols]
                new = jnp.maximum(old, top)
                fade = jnp.exp(old - new)
                exps = jnp.exp(scores - jnp.tile(new, (1, tk // HD)))
                l_s[:, cols] = l_s[:, cols] * fade + jnp.sum(exps, axis=1, keepdims=True)
                acc_s[:, cols] = acc_s[:, cols] * fade + dot(exps.astype(BF16), values)
                m_s[:, cols] = new

    step(high_block, True)

    def body(i, _):
        step(high_block - i, False)
        return 0

    lax.fori_loop(1, high_block - low_block + 1, body, 0)
    lane = lax.broadcasted_iota(jnp.int32, (tq, HD), 1)
    logs = jnp.zeros((tq, HD), F32)
    for h in range(heads):
        cols = slice(h * HD, (h + 1) * HD)
        total = l_s[:, cols]
        ctx[:, cols] = (acc_s[:, cols] / total).astype(BF16)
        logs = jnp.where(lane == h, m_s[:, cols] + jnp.log(total), logs)
    lse[...] = logs


def attend_forward(start, q, kv, seg_q, seg_k):
    rows, width = q.shape
    heads = width // HD
    tq = tk = 256
    length = kv.shape[0]
    return pl.pallas_call(
        functools.partial(attend_forward_kernel, tq=tq, tk=tk, heads=heads),
        grid=(rows // tq,),
        in_specs=[
            pl.BlockSpec(memory_space=pltpu.SMEM),
            pl.BlockSpec((tq, width), lambda i: (i, 0)),
            pl.BlockSpec((length, 2 * HD), lambda i: (0, 0)),
            pl.BlockSpec((tq, 1), lambda i: (i, 0)),
            pl.BlockSpec((1, length), lambda i: (0, 0)),
        ],
        out_specs=[
            pl.BlockSpec((tq, width), lambda i: (i, 0)),
            pl.BlockSpec((tq, HD), lambda i: (i, 0)),
        ],
        out_shape=[
            jax.ShapeDtypeStruct((rows, width), BF16),
            jax.ShapeDtypeStruct((rows, HD), F32),
        ],
        scratch_shapes=[
            pltpu.VMEM((tq, width), F32),
            pltpu.VMEM((tq, width), F32),
            pltpu.VMEM((tq, width), F32),
        ],
        compiler_params=pltpu.CompilerParams(vmem_limit_bytes=VMEM_BYTES),
        name="attend_forward",
    )(start, q, kv, seg_q, seg_k)


def attend_backward_kernel(
    start, q, kv, seg_q, seg_k, ctx, lse, dctx, dq, dkv, dq_s, *, tq, tk, heads
):
    first_query = start[0] + pl.program_id(0) * tq
    query_segs = seg_q[...]
    low_block = first_block(first_query, query_segs, seg_k[...], tk)
    high_block = lax.div(first_query + tq - 1, tk)
    scale = 1.0 / math.sqrt(HD)

    @pl.when(pl.program_id(0) == 0)
    def _():
        dkv[...] = jnp.zeros_like(dkv)

    dq_s[...] = jnp.zeros_like(dq_s)
    logs = lse[...]

    def body(i, _):
        first_key = pl.multiple_of((high_block - i) * tk, tk)
        keys = kv[pl.ds(first_key, tk), :HD]
        values = kv[pl.ds(first_key, tk), HD:]
        bias = block_bias(first_query, first_key, tq, tk, query_segs, seg_k[:, pl.ds(first_key, tk)])
        dk = jnp.zeros((tk, HD), F32)
        dv = jnp.zeros((tk, HD), F32)
        for h in range(heads):
            cols = slice(h * HD, (h + 1) * HD)
            q_h = q[:, cols]
            do_h = dctx[:, cols]
            inner = jnp.sum(do_h.astype(F32) * ctx[:, cols].astype(F32), axis=1, keepdims=True)
            scores = dot_t(q_h, keys) * scale + bias
            probs = jnp.exp(scores - logs[:, h : h + 1])
            dprobs = dot_t(do_h, values)
            dscores = (probs * (dprobs - inner)).astype(BF16)
            dq_s[:, cols] += dot(dscores, keys)
            dk = dk + t_dot(dscores, q_h)
            dv = dv + t_dot(probs.astype(BF16), do_h)
        dkv[pl.ds(first_key, tk), :HD] += dk * scale
        dkv[pl.ds(first_key, tk), HD:] += dv
        return 0

    lax.fori_loop(0, high_block - low_block + 1, body, 0)
    dq[...] = (dq_s[...] * scale).astype(BF16)


def attend_backward(start, q, kv, seg_q, seg_k, ctx, lse, dctx):
    rows, width = q.shape
    heads = width // HD
    tq = tk = 256
    length = kv.shape[0]
    return pl.pallas_call(
        functools.partial(attend_backward_kernel, tq=tq, tk=tk, heads=heads),
        grid=(rows // tq,),
        in_specs=[
            pl.BlockSpec(memory_space=pltpu.SMEM),
            pl.BlockSpec((tq, width), lambda i: (i, 0)),
            pl.BlockSpec((length, 2 * HD), lambda i: (0, 0)),
            pl.BlockSpec((tq, 1), lambda i: (i, 0)),
            pl.BlockSpec((1, length), lambda i: (0, 0)),
            pl.BlockSpec((tq, width), lambda i: (i, 0)),
            pl.BlockSpec((tq, HD), lambda i: (i, 0)),
            pl.BlockSpec((tq, width), lambda i: (i, 0)),
        ],
        out_specs=[
            pl.BlockSpec((tq, width), lambda i: (i, 0)),
            pl.BlockSpec((length, 2 * HD), lambda i: (0, 0)),
        ],
        out_shape=[
            jax.ShapeDtypeStruct((rows, width), BF16),
            jax.ShapeDtypeStruct((length, 2 * HD), F32),
        ],
        scratch_shapes=[pltpu.VMEM((tq, width), F32)],
        compiler_params=pltpu.CompilerParams(vmem_limit_bytes=VMEM_BYTES),
        name="attend_backward",
    )(start, q, kv, seg_q, seg_k, ctx, lse, dctx)


def feed_kernel(n2, dy, wg, wu, wd, hidden, dgate, dup):
    gate = dot(n2[...], wg[...])
    up = dot(n2[...], wu[...])
    dh = dot_t(dy[...], wd[...])
    root = math.sqrt(2.0 / math.pi)
    square = gate * gate
    tanh = jnp.tanh(root * (gate + 0.044715 * gate * square))
    half = 0.5 * (1.0 + tanh)
    act = gate * half
    slope = half + 0.5 * gate * (1.0 - tanh * tanh) * (root * (1.0 + 3.0 * 0.044715 * square))
    hidden[...] = (act * up).astype(BF16)
    dgate[...] = (dh * up * slope).astype(BF16)
    dup[...] = (dh * act).astype(BF16)


def feed(n2, dy, wg, wu, wd):
    rows, width = n2.shape
    units = wg.shape[1]
    tm, tn = 512, 384
    out = jax.ShapeDtypeStruct((rows, units), BF16)
    return pl.pallas_call(
        feed_kernel,
        grid=(units // tn, rows // tm),
        in_specs=[
            pl.BlockSpec((tm, width), lambda j, i: (i, 0)),
            pl.BlockSpec((tm, width), lambda j, i: (i, 0)),
            pl.BlockSpec((width, tn), lambda j, i: (0, j)),
            pl.BlockSpec((width, tn), lambda j, i: (0, j)),
            pl.BlockSpec((tn, width), lambda j, i: (j, 0)),
        ],
        out_specs=[pl.BlockSpec((tm, tn), lambda j, i: (i, j))] * 3,
        out_shape=[out] * 3,
        compiler_params=pltpu.CompilerParams(vmem_limit_bytes=VMEM_BYTES),
        name="feed",
    )(n2, dy, wg, wu, wd)


def per_device(
    tokens_in,
    norm1_gain,
    w_query,
    w_keyval,
    w_attn_out,
    norm2_gain,
    w_gate,
    w_up,
    w_down,
    segment_ids,
    out_cotangent,
):
    width = D
    row = lax.axis_index("row")
    col = lax.axis_index("col")
    local = tokens_in.shape[0]
    mine = local // 2
    feats = tokens_in.shape[1]
    length = segment_ids.shape[1]
    spans = length // local

    def keep(value):
        return lax.dynamic_slice_in_dim(value, row * mine, mine, 0)

    def give(value):
        return lax.dynamic_slice_in_dim(value, (1 - row) * mine, mine, 0)

    x_in = swap_row(give(tokens_in))
    gains = jnp.stack([norm1_gain, norm2_gain])
    gains_in = swap_row(gains)
    gain_one = jnp.concatenate([norm1_gain, gains_in[0]])
    gain_two = jnp.concatenate([norm2_gain, gains_in[1]])
    segs_in = swap_row(segment_ids)
    is_low = row == 0
    segs_all = jnp.concatenate(
        [jnp.where(is_low, segment_ids, segs_in), jnp.where(is_low, segs_in, segment_ids)], axis=0
    )
    wkv_in = swap_row(w_keyval)
    wq_in = swap_row(w_query)
    wo_in = swap_row(after(w_attn_out, wq_in))
    dy_in = swap_row(after(give(out_cotangent), wo_in))
    wg_in = swap_row(after(w_gate, dy_in))
    wu_in = swap_row(after(w_up, wg_in))
    wd_in = swap_row(after(w_down, wu_in))

    wq_own = jnp.concatenate([w_query, wq_in], axis=0)
    wo_own = jnp.concatenate([w_attn_out, wo_in], axis=1)
    wq_all = jnp.concatenate(gather_col(wq_own), axis=1)
    wo_all = jnp.concatenate(gather_col(after(wo_own, wq_all)), axis=0)
    wkv = jnp.concatenate([w_keyval, wkv_in], axis=0)
    wg = jnp.concatenate([w_gate, wg_in], axis=0)
    wu = jnp.concatenate([w_up, wu_in], axis=0)
    wd = jnp.concatenate([w_down, wd_in], axis=1)

    x = jnp.concatenate([keep(tokens_in), x_in], axis=1).astype(F32)
    inverse_one = lax.rsqrt(jnp.mean(x * x, axis=1, keepdims=True) + EPSILON)
    normed_one = (x * inverse_one * gain_one).astype(BF16)
    kv_own = dot(normed_one, wkv, BF16)
    kv_in = swap_row(kv_own)
    kv_pair = jnp.concatenate(
        [jnp.where(is_low, kv_own, kv_in), jnp.where(is_low, kv_in, kv_own)], axis=0
    )
    place = col % spans
    if spans == 2:
        kv_far = swap_core(kv_pair)
        first = place == 0
        kv = jnp.concatenate(
            [jnp.where(first, kv_pair, kv_far), jnp.where(first, kv_far, kv_pair)], axis=0
        )
    else:
        kv = kv_pair
    seg_row = lax.dynamic_slice_in_dim(segs_all, col // spans, 1, 0)
    first_token = place * local + row * mine
    seg_q = lax.dynamic_slice_in_dim(seg_row[0], first_token, mine, 0)[:, None]
    start = jnp.reshape(first_token, (1,)).astype(jnp.int32)

    q = dot(normed_one, wq_all, BF16)
    ctx, lse = attend_forward(start, q, kv, seg_q, seg_row)
    middle = x + dot(ctx, wo_all)
    inverse_two = lax.rsqrt(jnp.mean(middle * middle, axis=1, keepdims=True) + EPSILON)
    normed_two = (middle * inverse_two * gain_two).astype(BF16)

    dy = jnp.concatenate([keep(out_cotangent), dy_in], axis=1)
    dy_all = jnp.concatenate(gather_col(dy), axis=0)
    n2_all = jnp.concatenate(gather_col(normed_two), axis=0)
    hidden, dgate, dup = feed(n2_all, dy_all, wg, wu, wd)
    dn2 = dot_t(dgate, wg) + dot_t(dup, wu)
    dn2 = dn2.astype(BF16)
    down_part = t_dot(hidden, dy_all, BF16)
    gate_part = t_dot(n2_all, dgate, BF16)
    up_part = t_dot(n2_all, dup, BF16)
    ffn = dot(hidden, wd, BF16)

    def rows_from_row(part):
        return part[:feats] + swap_row(part[feats:])

    def cols_from_row(part):
        return part[:, :feats] + swap_row(part[:, feats:])

    down_total = total_over_dp(cols_from_row(down_part))
    gate_total = total_over_dp(rows_from_row(gate_part))
    up_total = total_over_dp(rows_from_row(up_part))

    def blocks(value):
        return [value[i * mine : (i + 1) * mine] for i in range(4)]

    dnormed_two = scatter_col(*blocks(dn2))
    scaled = dnormed_two * gain_two
    projection = jnp.mean(scaled * middle, axis=1, keepdims=True)
    dmiddle = dy.astype(F32) + inverse_two * scaled - middle * (inverse_two**3 * projection)
    gain_two_part = jnp.sum(dnormed_two * middle * inverse_two, axis=0)

    dattn = dmiddle.astype(BF16)
    dctx = dot_t(dattn, wo_all, BF16)
    dq, dkv_all = attend_backward(start, q, kv, seg_q, seg_row, ctx, lse, dctx)
    if spans == 2:
        low_half, high_half = dkv_all[:local], dkv_all[local:]
        ours = jnp.where(place == 0, low_half, high_half)
        theirs = jnp.where(place == 0, high_half, low_half)
        dkv_pair = ours + swap_core(theirs.astype(BF16)).astype(F32)
    else:
        dkv_pair = dkv_all
    dkv = keep(dkv_pair) + swap_row(give(dkv_pair).astype(BF16)).astype(F32)
    dkv = dkv.astype(BF16)
    dnormed_one = dot_t(dq, wq_all) + dot_t(dkv, wkv)
    scaled = dnormed_one * gain_one
    projection = jnp.mean(scaled * x, axis=1, keepdims=True)
    dx = dmiddle + inverse_one * scaled - x * (inverse_one**3 * projection)
    gain_one_part = jnp.sum(dnormed_one * x * inverse_one, axis=0)

    heads_own = w_query.shape[1]

    def scatter_four(parts):
        return scatter_col(*parts).astype(BF16)

    out_part = t_dot(ctx, dattn, BF16)
    out_mine = scatter_four([out_part[i * heads_own : (i + 1) * heads_own] for i in range(4)])
    out_total = total_over_dp(cols_from_row(out_mine))
    query_part = t_dot(normed_one, dq, BF16)
    query_mine = scatter_four([query_part[:, i * heads_own : (i + 1) * heads_own] for i in range(4)])
    query_total = total_over_dp(rows_from_row(query_mine))
    kv_part = t_dot(normed_one, dkv)
    kv_mine = rows_from_row(kv_part)
    gain_parts = jnp.stack([gain_one_part, gain_two_part], axis=1)
    gain_mine = rows_from_row(gain_parts)
    kv_total, gain_total = lax.psum((kv_mine, gain_mine), ("dp", "col"))

    ffn_own = scatter_col(*blocks(ffn))
    y = middle + ffn_own

    def put_back(value):
        other = swap_row(value[:, feats:].astype(BF16)).astype(F32)
        own = value[:, :feats]
        return jnp.concatenate(
            [jnp.where(is_low, own, other), jnp.where(is_low, other, own)], axis=0
        )

    return (
        put_back(y),
        put_back(dx),
        query_total,
        kv_total,
        out_total,
        gate_total,
        up_total,
        down_total,
        gain_total[:, 0],
        gain_total[:, 1],
    )


def solution(mesh):
    return jax.shard_map(
        per_device,
        mesh=mesh,
        in_specs=(
            P(("dp", "col"), "row"),
            P("row"),
            P("row", "col"),
            P("row", None),
            P("col", "row"),
            P("row"),
            P("row", "col"),
            P("row", "col"),
            P("col", "row"),
            P(("dp", "row"), None),
            P(("dp", "col"), "row"),
        ),
        out_specs=(
            P(("dp", "col"), "row"),
            P(("dp", "col"), "row"),
            P("row", "col"),
            P("row", None),
            P("col", "row"),
            P("row", "col"),
            P("row", "col"),
            P("col", "row"),
            P("row"),
            P("row"),
        ),
        check_vma=False,
    )
```

```python
import functools
import math

import jax
import jax.numpy as jnp
from jax import lax
from jax.experimental import pallas as pl
from jax.experimental.pallas import tpu as pltpu
from jax.sharding import PartitionSpec as P

D = 1536
HD = 128
WINDOW = 1024
EPSILON = 1e-06
NEGATIVE = -1e30
BF16 = jnp.bfloat16
F32 = jnp.float32
VMEM_BYTES = 56 * 1024 * 1024
HEAVY = pl.CostEstimate(flops=10**12, bytes_accessed=10**9, transcendentals=0)


def after(value, *earlier):
    return lax.optimization_barrier((value, *earlier))[0]


def swap_row(value):
    return lax.ppermute(value, "row", [(0, 1), (1, 0)])


def swap_core(value):
    return lax.ppermute(value, "col", [(0, 1), (1, 0), (2, 3), (3, 2)])


def swap_far(value):
    return lax.ppermute(value, "col", [(0, 2), (2, 0), (1, 3), (3, 1)])


def dot(left, right, out=F32):
    return jnp.dot(left, right, preferred_element_type=F32).astype(out)


def dot_t(left, right, out=F32):
    return lax.dot_general(
        left, right, (((1,), (1,)), ((), ())), preferred_element_type=F32
    ).astype(out)


def t_dot(left, right, out=F32):
    return lax.dot_general(
        left, right, (((0,), (0,)), ((), ())), preferred_element_type=F32
    ).astype(out)


def swap_pair(value):
    count = lax.axis_size("dp")
    return lax.ppermute(value, "dp", [(i, i ^ 1) for i in range(count)])


def swap_mirror(value):
    count = lax.axis_size("dp")
    return lax.ppermute(value, "dp", [(i, count - 1 - i) for i in range(count)])


class Steps:
    def __init__(self):
        self.last = ()

    def __call__(self, function, first, *rest):
        result = function(after(first, *self.last) if self.last else first, *rest)
        self.last = tuple(result) if isinstance(result, (tuple, list)) else (result,)
        return result


class DpTotal:
    def __init__(self, steps):
        self.steps = steps
        self.staged = lax.axis_size("dp") == 4
        self.side = (lax.axis_index("dp") + 1) // 2 % 2

    def begin(self, own, other):
        if not self.staged:
            self.value = lax.psum(own + other, "dp")
            return
        span = own.shape[0] // 2

        def both(other):
            def half(which):
                at = which * span
                return lax.dynamic_slice_in_dim(own, at, span, 0) + lax.dynamic_slice_in_dim(
                    other, at, span, 0
                )

            return half(1 - self.side), half(self.side)

        give, self.keep = self.steps(both, other)
        self.inward = swap_pair(give)

    def middle(self):
        if self.staged:
            self.pair = self.steps(jnp.add, self.inward, self.keep)
            self.across = swap_mirror(self.pair)

    def end(self):
        if self.staged:
            self.total = self.steps(jnp.add, self.across, self.pair)
            self.rest = swap_pair(self.total)

    def result(self):
        if not self.staged:
            return self.value.astype(F32)
        first = self.side == 0

        def join(rest):
            return jnp.concatenate(
                [jnp.where(first, self.total, rest), jnp.where(first, rest, self.total)], axis=0
            ).astype(F32)

        return self.steps(join, self.rest)


def fence_kernel(value, out):
    out[...] = value[...]


class Rounds:
    def __init__(self):
        self.token = jnp.zeros((8, 128), F32)

    def send(self, move, value):
        return move(after(value, self.token))

    def wait(self, *results):
        token = pl.pallas_call(
            fence_kernel,
            out_shape=jax.ShapeDtypeStruct((8, 128), F32),
            cost_estimate=HEAVY,
            name="fence",
        )(self.token)
        self.token = after(token, *results)


def place_kernel(odd, straight, around, out):
    is_straight = pl.program_id(0) == odd[0]

    @pl.when(is_straight)
    def _():
        out[...] = straight[...]

    @pl.when(jnp.logical_not(is_straight))
    def _():
        out[...] = around[...]


def place_rows(odd, straight, around):
    rows, cols = straight.shape
    whole = pl.BlockSpec((rows, cols), lambda i: (0, 0))
    return pl.pallas_call(
        place_kernel,
        grid=(2,),
        in_specs=[pl.BlockSpec(memory_space=pltpu.SMEM), whole, whole],
        out_specs=pl.BlockSpec((rows, cols), lambda i: (i, 0)),
        out_shape=jax.ShapeDtypeStruct((2 * rows, cols), straight.dtype),
        compiler_params=pltpu.CompilerParams(vmem_limit_bytes=VMEM_BYTES),
        cost_estimate=HEAVY,
        name="place_rows",
    )(jnp.reshape(odd, (1,)).astype(jnp.int32), straight, around)


def block_bias(first_query, first_key, rows, cols, query_segs, key_segs):
    query_pos = first_query + lax.broadcasted_iota(jnp.int32, (rows, cols), 0)
    key_pos = first_key + lax.broadcasted_iota(jnp.int32, (rows, cols), 1)
    distance = query_pos - key_pos
    allowed = (query_segs == key_segs) & (distance >= 0) & (distance < WINDOW)
    return jnp.where(allowed, 0.0, NEGATIVE)


def first_block(first_query, query_segs, key_segs, tile_k):
    earlier = jnp.sum((key_segs < query_segs[0:1, 0:1]).astype(jnp.int32))
    return lax.div(jnp.maximum(earlier, first_query - (WINDOW - 1)), tile_k)


def attend_forward_kernel(
    start, q_a, q_b, kv, seg_q, seg_k, ctx_a, ctx_b, lse, m_s, l_s, acc_s, *, tq, tk, heads
):
    first_query = start[0] + pl.program_id(0) * tq
    query_segs = seg_q[...]
    low_block = first_block(first_query, query_segs, seg_k[...], tk)
    high_block = lax.div(first_query + tq - 1, tk)
    scale = 1.0 / math.sqrt(HD)

    def step(block, first):
        first_key = pl.multiple_of(block * tk, tk)
        keys = kv[pl.ds(first_key, tk), :HD]
        values = kv[pl.ds(first_key, tk), HD:]
        bias = block_bias(first_query, first_key, tq, tk, query_segs, seg_k[:, pl.ds(first_key, tk)])
        for h in range(2 * heads):
            q = (q_a, q_b)[h // heads]
            own = slice(h % heads * HD, (h % heads + 1) * HD)
            cols = slice(h * HD, (h + 1) * HD)
            scores = dot_t(q[:, own], keys) * scale + bias
            top = jnp.max(scores, axis=1, keepdims=True)
            if first:
                exps = jnp.exp(scores - top)
                l_s[:, cols] = jnp.broadcast_to(jnp.sum(exps, axis=1, keepdims=True), (tq, HD))
                acc_s[:, cols] = dot(exps.astype(BF16), values)
                m_s[:, cols] = jnp.broadcast_to(top, (tq, HD))
            else:
                old = m_s[:, cols]
                new = jnp.maximum(old, top)
                fade = jnp.exp(old - new)
                exps = jnp.exp(scores - jnp.tile(new, (1, tk // HD)))
                l_s[:, cols] = l_s[:, cols] * fade + jnp.sum(exps, axis=1, keepdims=True)
                acc_s[:, cols] = acc_s[:, cols] * fade + dot(exps.astype(BF16), values)
                m_s[:, cols] = new

    step(high_block, True)

    def body(i, _):
        step(high_block - i, False)
        return 0

    lax.fori_loop(1, high_block - low_block + 1, body, 0)
    lane = lax.broadcasted_iota(jnp.int32, (tq, HD), 1)
    logs = jnp.zeros((tq, HD), F32)
    for h in range(2 * heads):
        own = slice(h % heads * HD, (h % heads + 1) * HD)
        cols = slice(h * HD, (h + 1) * HD)
        total = l_s[:, cols]
        (ctx_a, ctx_b)[h // heads][:, own] = (acc_s[:, cols] / total).astype(BF16)
        logs = jnp.where(lane == h, m_s[:, cols] + jnp.log(total), logs)
    lse[...] = logs


def attend_forward(start, q_a, q_b, kv, seg_q, seg_k):
    rows, width = q_a.shape
    tq = tk = 256
    length = kv.shape[0]
    tile = pl.BlockSpec((tq, width), lambda i: (i, 0))
    ctx = jax.ShapeDtypeStruct((rows, width), BF16)
    return pl.pallas_call(
        functools.partial(attend_forward_kernel, tq=tq, tk=tk, heads=width // HD),
        grid=(rows // tq,),
        in_specs=[
            pl.BlockSpec(memory_space=pltpu.SMEM),
            tile,
            tile,
            pl.BlockSpec((length, 2 * HD), lambda i: (0, 0)),
            pl.BlockSpec((tq, 1), lambda i: (i, 0)),
            pl.BlockSpec((1, length), lambda i: (0, 0)),
        ],
        out_specs=[tile, tile, pl.BlockSpec((tq, HD), lambda i: (i, 0))],
        out_shape=[ctx, ctx, jax.ShapeDtypeStruct((rows, HD), F32)],
        scratch_shapes=[pltpu.VMEM((tq, 2 * width), F32)] * 3,
        compiler_params=pltpu.CompilerParams(vmem_limit_bytes=VMEM_BYTES),
        cost_estimate=HEAVY,
        name="attend_forward",
    )(start, q_a, q_b, kv, seg_q, seg_k)


def attend_backward_kernel(
    start, q_a, q_b, kv, seg_q, seg_k, ctx_a, ctx_b, lse, dctx_a, dctx_b, dq_a, dq_b, dkv, dq_s,
    *, tq, tk, heads,
):
    first_query = start[0] + pl.program_id(0) * tq
    query_segs = seg_q[...]
    low_block = first_block(first_query, query_segs, seg_k[...], tk)
    high_block = lax.div(first_query + tq - 1, tk)
    scale = 1.0 / math.sqrt(HD)

    @pl.when(pl.program_id(0) == 0)
    def _():
        dkv[...] = jnp.zeros_like(dkv)

    dq_s[...] = jnp.zeros_like(dq_s)
    logs = lse[...]

    def body(i, _):
        first_key = pl.multiple_of((high_block - i) * tk, tk)
        keys = kv[pl.ds(first_key, tk), :HD]
        values = kv[pl.ds(first_key, tk), HD:]
        bias = block_bias(first_query, first_key, tq, tk, query_segs, seg_k[:, pl.ds(first_key, tk)])
        dk = jnp.zeros((tk, HD), F32)
        dv = jnp.zeros((tk, HD), F32)
        for h in range(2 * heads):
            own = slice(h % heads * HD, (h % heads + 1) * HD)
            cols = slice(h * HD, (h + 1) * HD)
            q_h = (q_a, q_b)[h // heads][:, own]
            do_h = (dctx_a, dctx_b)[h // heads][:, own]
            ctx_h = (ctx_a, ctx_b)[h // heads][:, own]
            inner = jnp.sum(do_h.astype(F32) * ctx_h.astype(F32), axis=1, keepdims=True)
            scores = dot_t(q_h, keys) * scale + bias
            probs = jnp.exp(scores - logs[:, h : h + 1])
            dprobs = dot_t(do_h, values)
            dscores = (probs * (dprobs - inner)).astype(BF16)
            dq_s[:, cols] += dot(dscores, keys)
            dk = dk + t_dot(dscores, q_h)
            dv = dv + t_dot(probs.astype(BF16), do_h)
        dkv[pl.ds(first_key, tk), :HD] += dk * scale
        dkv[pl.ds(first_key, tk), HD:] += dv
        return 0

    lax.fori_loop(0, high_block - low_block + 1, body, 0)
    half = heads * HD
    dq_a[...] = (dq_s[:, :half] * scale).astype(BF16)
    dq_b[...] = (dq_s[:, half:] * scale).astype(BF16)


def attend_backward(start, q_a, q_b, kv, seg_q, seg_k, ctx_a, ctx_b, lse, dctx_a, dctx_b):
    rows, width = q_a.shape
    tq = tk = 256
    length = kv.shape[0]
    tile = pl.BlockSpec((tq, width), lambda i: (i, 0))
    dq = jax.ShapeDtypeStruct((rows, width), BF16)
    return pl.pallas_call(
        functools.partial(attend_backward_kernel, tq=tq, tk=tk, heads=width // HD),
        grid=(rows // tq,),
        in_specs=[
            pl.BlockSpec(memory_space=pltpu.SMEM),
            tile,
            tile,
            pl.BlockSpec((length, 2 * HD), lambda i: (0, 0)),
            pl.BlockSpec((tq, 1), lambda i: (i, 0)),
            pl.BlockSpec((1, length), lambda i: (0, 0)),
            tile,
            tile,
            pl.BlockSpec((tq, HD), lambda i: (i, 0)),
            tile,
            tile,
        ],
        out_specs=[tile, tile, pl.BlockSpec((length, 2 * HD), lambda i: (0, 0))],
        out_shape=[dq, dq, jax.ShapeDtypeStruct((length, 2 * HD), F32)],
        scratch_shapes=[pltpu.VMEM((tq, 2 * width), F32)],
        compiler_params=pltpu.CompilerParams(vmem_limit_bytes=VMEM_BYTES),
        cost_estimate=HEAVY,
        name="attend_backward",
    )(start, q_a, q_b, kv, seg_q, seg_k, ctx_a, ctx_b, lse, dctx_a, dctx_b)


def feed_kernel(
    n2_a, n2_b, dy_a, dy_b, dy_c, dy_d, wg_a, wg_b, wu_a, wu_b, wd_a, wd_b, hidden, dgate, dup, *, tm
):
    root = math.sqrt(2.0 / math.pi)
    rows = n2_a.shape[0]
    feats = wg_a.shape[0]
    for base, n2, first_dy, second_dy in ((0, n2_a, dy_a, dy_b), (rows, n2_b, dy_c, dy_d)):
        for first in range(0, rows, tm):
            own = slice(first, first + tm)
            low, high = n2[own, :feats], n2[own, feats:]
            gate = dot(low, wg_a[...]) + dot(high, wg_b[...])
            up = dot(low, wu_a[...]) + dot(high, wu_b[...])
            dh = dot_t(first_dy[own], wd_a[...]) + dot_t(second_dy[own], wd_b[...])
            square = gate * gate
            tanh = jnp.tanh(gate * (root + (root * 0.044715) * square))
            half = 0.5 + 0.5 * tanh
            act = gate * half
            slope = half + act * (1.0 - tanh) * (root + (3.0 * 0.044715 * root) * square)
            out = slice(base + first, base + first + tm)
            hidden[out] = (act * up).astype(BF16)
            dgate[out] = (dh * up * slope).astype(BF16)
            dup[out] = (dh * act).astype(BF16)


def feed(n2s, dys, wg, wu, wd):
    rows, width = n2s[0].shape
    feats, units = wg[0].shape
    tn = 384
    whole = pl.BlockSpec((rows, width), lambda j: (0, 0))
    half = pl.BlockSpec((rows, feats), lambda j: (0, 0))
    out = jax.ShapeDtypeStruct((2 * rows, units), BF16)
    return pl.pallas_call(
        functools.partial(feed_kernel, tm=256),
        grid=(units // tn,),
        in_specs=[whole] * 2
        + [half] * 4
        + [pl.BlockSpec((feats, tn), lambda j: (0, j))] * 4
        + [pl.BlockSpec((tn, feats), lambda j: (j, 0))] * 2,
        out_specs=[pl.BlockSpec((2 * rows, tn), lambda j: (0, j))] * 3,
        out_shape=[out] * 3,
        compiler_params=pltpu.CompilerParams(vmem_limit_bytes=VMEM_BYTES),
        cost_estimate=HEAVY,
        name="feed",
    )(*n2s, *dys, *wg, *wu, *wd)


def weight_grad_kernel(*refs):
    out = refs[-1]
    pairs = len(refs) // 2
    total = None
    for left, right in zip(refs[:pairs], refs[pairs:-1]):
        part = t_dot(left[...], right[...])
        total = part if total is None else total + part
    out[...] = total.astype(BF16)


def weight_grad(lefts, rights, name):
    width_left = lefts[0][4]
    width_right = rights[0][4]
    tn = 384

    def left_spec(block):
        _, at, rows, col, cols = block
        return pl.BlockSpec((rows, cols), lambda j: (at, col))

    def right_spec(block):
        _, at, rows, col, cols = block
        return pl.BlockSpec((rows, tn), lambda j: (at, col * (cols // tn) + j))

    out = jax.ShapeDtypeStruct((width_left, width_right), BF16)
    tokens = sum(block[2] for block in lefts)
    return pl.pallas_call(
        weight_grad_kernel,
        grid=(width_right // tn,),
        in_specs=[left_spec(b) for b in lefts] + [right_spec(b) for b in rights],
        out_specs=pl.BlockSpec((width_left, tn), lambda j: (0, j)),
        out_shape=out,
        compiler_params=pltpu.CompilerParams(vmem_limit_bytes=VMEM_BYTES),
        cost_estimate=HEAVY,
        name=name,
    )(*[b[0] for b in lefts], *[b[0] for b in rights])


def project_kernel(*refs, lefts, multiply):
    left = refs[:lefts]
    weights = refs[lefts : 3 * lefts]
    first, second = refs[3 * lefts :]
    rows = first.shape[0]
    in_first = pl.program_id(0) < pl.num_programs(0) // 2

    def fill(chosen):
        for at, out in ((0, first), (rows, second)):
            own = slice(at, at + rows)
            out[...] = sum(multiply(l[own], w[...]) for l, w in zip(left, chosen)).astype(BF16)

    pl.when(in_first)(lambda: fill(weights[0::2]))
    pl.when(jnp.logical_not(in_first))(lambda: fill(weights[1::2]))


def project(lefts, weights, transposed, name):
    rows, units = lefts[0].shape
    feats = weights[0][0].shape[0 if transposed else 1]
    tn = 384
    tiles = feats // tn
    whole = pl.BlockSpec((rows, units), lambda j: (0, 0))

    def low(j):
        return jnp.minimum(j, tiles - 1)

    def high(j):
        return jnp.maximum(j - tiles, 0)

    if transposed:
        specs = [pl.BlockSpec((tn, units), lambda j, f=f: (f(j), 0)) for f in (low, high)]
    else:
        specs = [pl.BlockSpec((units, tn), lambda j, f=f: (0, f(j))) for f in (low, high)]
    out = jax.ShapeDtypeStruct((rows // 2, 2 * feats), BF16)
    flat = [half for weight in weights for half in weight]
    return pl.pallas_call(
        functools.partial(
            project_kernel, lefts=len(lefts), multiply=dot_t if transposed else dot
        ),
        grid=(2 * tiles,),
        in_specs=[whole] * len(lefts) + specs * len(lefts),
        out_specs=[pl.BlockSpec((rows // 2, tn), lambda j: (0, j))] * 2,
        out_shape=[out] * 2,
        compiler_params=pltpu.CompilerParams(vmem_limit_bytes=VMEM_BYTES),
        cost_estimate=HEAVY,
        name=name,
    )(*lefts, *flat)


def per_device(
    tokens_in,
    norm1_gain,
    w_query,
    w_keyval,
    w_attn_out,
    norm2_gain,
    w_gate,
    w_up,
    w_down,
    segment_ids,
    out_cotangent,
):
    width = D
    row = lax.axis_index("row")
    col = lax.axis_index("col")
    local = tokens_in.shape[0]
    mine = local // 2
    feats = tokens_in.shape[1]
    length = segment_ids.shape[1]
    spans = length // local

    def keep(value):
        return lax.dynamic_slice_in_dim(value, row * mine, mine, 0)

    def give(value):
        return lax.dynamic_slice_in_dim(value, (1 - row) * mine, mine, 0)

    is_low = row == 0

    odd = lax.axis_index("dp") % 2
    paired = lax.axis_size("dp") % 2 == 0

    def straight_part(weight):
        span = weight.shape[0] // 2
        return lax.dynamic_slice_in_dim(weight, odd * span, span, 0) if paired else weight

    def placed(straight, around):
        return place_rows(odd, straight, around) if paired else straight

    def send_pair(straight):
        return rounds.send(swap_pair, straight) if paired else straight

    rounds = Rounds()
    small = jnp.concatenate([norm1_gain, norm2_gain, segment_ids.reshape(-1).astype(F32)])
    w_qkv = jnp.concatenate([w_query, w_keyval], axis=1)
    heads_own = w_query.shape[1]
    x_in = rounds.send(swap_row, give(tokens_in))
    wq_far_own = rounds.send(swap_far, w_query)
    small_in = rounds.send(swap_row, small)
    wqkv_in = rounds.send(swap_row, w_qkv)
    rounds.wait(x_in, wq_far_own, small_in)

    wo_far_own = rounds.send(swap_far, w_attn_out)
    wo_in = rounds.send(swap_row, w_attn_out)
    gain_one = jnp.concatenate([norm1_gain, small_in[:feats]])
    gain_two = jnp.concatenate([norm2_gain, small_in[feats : 2 * feats]])
    segs_in = small_in[2 * feats :].astype(jnp.int32).reshape(segment_ids.shape)
    segs_all = jnp.concatenate(
        [jnp.where(is_low, segment_ids, segs_in), jnp.where(is_low, segs_in, segment_ids)], axis=0
    )
    x = jnp.concatenate([keep(tokens_in), x_in], axis=1).astype(F32)
    inverse_one = lax.rsqrt(jnp.mean(x * x, axis=1, keepdims=True) + EPSILON)
    normed_one = (x * inverse_one * gain_one).astype(BF16)
    place = col % spans
    seg_row = lax.dynamic_slice_in_dim(segs_all, col // spans, 1, 0)
    first_token = place * local + row * mine
    seg_q = lax.dynamic_slice_in_dim(seg_row[0], first_token, mine, 0)[:, None]
    start = jnp.reshape(first_token, (1,)).astype(jnp.int32)
    rounds.wait(wqkv_in, wo_far_own)

    wq_in = wqkv_in[:, :heads_own]
    wq_far_in = rounds.send(swap_far, wq_in)
    wkv = jnp.concatenate([w_keyval, wqkv_in[:, heads_own:]], axis=0)
    kv_own = dot(normed_one, wkv, BF16)
    kv_in = rounds.send(swap_row, kv_own)
    wg_straight = rounds.send(swap_row, after(straight_part(w_gate), kv_own))
    rounds.wait(wo_in, kv_in, wq_far_in)

    kv_pair = jnp.concatenate(
        [jnp.where(is_low, kv_own, kv_in), jnp.where(is_low, kv_in, kv_own)], axis=0
    )
    wq_half = jnp.concatenate(
        [
            jnp.concatenate([w_query, wq_far_own], axis=1),
            jnp.concatenate([wq_in, wq_far_in], axis=1),
        ],
        axis=0,
    )
    wo_far_in = rounds.send(swap_far, wo_in)
    wu_straight = rounds.send(swap_row, straight_part(w_up))
    wq_core = rounds.send(swap_core, wq_half)
    if spans == 2:
        kv_far = rounds.send(swap_core, kv_pair)
        first = place == 0
        kv = jnp.concatenate(
            [jnp.where(first, kv_pair, kv_far), jnp.where(first, kv_far, kv_pair)], axis=0
        )
    else:
        kv = kv_pair
    q_a = dot(normed_one, wq_half, BF16)
    q_b = dot(normed_one, wq_core, BF16)
    rounds.wait(wo_far_in, kv, q_b)

    wo_half = jnp.concatenate(
        [
            jnp.concatenate([w_attn_out, wo_far_own], axis=0),
            jnp.concatenate([wo_in, wo_far_in], axis=0),
        ],
        axis=1,
    )
    dy_own = keep(out_cotangent)
    wo_core = rounds.send(swap_core, wo_half)
    dy_far_own = rounds.send(swap_far, dy_own)
    ctx_a, ctx_b, lse = attend_forward(start, after(q_a, rounds.token), q_b, kv, seg_q, seg_row)
    middle = x + dot(ctx_a, wo_half) + dot(ctx_b, wo_core)
    inverse_two = lax.rsqrt(jnp.mean(middle * middle, axis=1, keepdims=True) + EPSILON)
    n2 = (middle * inverse_two * gain_two).astype(BF16)
    rounds.wait(wg_straight, n2)

    n2_far = rounds.send(swap_far, n2)
    wg_around = send_pair(wg_straight)
    wd_straight = rounds.send(swap_row, straight_part(w_down))
    n2_near = rounds.send(swap_core, n2)
    rounds.wait(wu_straight, wg_around, n2_near, dy_far_own)

    dy_in = rounds.send(swap_row, give(out_cotangent))
    wu_around = send_pair(wu_straight)
    dy_near_own = rounds.send(swap_core, dy_own)
    rounds.wait(wd_straight, wu_around, dy_near_own)

    wd_around = send_pair(wd_straight)
    dy_diagonal_own = rounds.send(swap_core, dy_far_own)
    wg = (w_gate, placed(wg_straight, wg_around))
    wu = (w_up, placed(wu_straight, wu_around))
    rounds.wait(dy_in, n2_far, dy_diagonal_own)

    dy_near_in = rounds.send(swap_core, dy_in)
    dy_far_in = rounds.send(swap_far, dy_in)
    n2_diagonal = rounds.send(swap_core, n2_far)
    wd = (w_down, placed(wd_straight, wd_around))
    dy_near = (dy_near_own, dy_near_in)
    hidden_a, dgate_a, dup_a = feed((n2, n2_near), (dy_own, dy_in, *dy_near), wg, wu, wd)
    dy_diagonal = (dy_diagonal_own, swap_core(dy_far_in))
    hidden_b, dgate_b, dup_b = feed(
        (after(n2_far, hidden_a), n2_diagonal), (dy_far_own, dy_far_in, *dy_diagonal), wg, wu, wd
    )

    normed = [n2, n2_near, n2_far, n2_diagonal]
    cotangents = [(dy_own, dy_in), dy_near, (dy_far_own, dy_far_in), dy_diagonal]
    units = w_gate.shape[1]

    def normed_blocks(half):
        return [(value, 0, mine, half, feats) for value in normed]

    def cotangent_blocks(half):
        return [(value[half], 0, mine, 0, feats) for value in cotangents]

    def unit_blocks(first_pair, second_pair, *earlier):
        if earlier:
            first_pair = after(first_pair, *earlier)
        return [
            (value, at, mine, 0, units) for value in (first_pair, second_pair) for at in range(2)
        ]

    steps = Steps()

    def gate_grad(half):
        return steps(
            lambda last: weight_grad(normed_blocks(half), unit_blocks(dgate_a, last), "w_gate_grad"),
            dgate_b,
        )

    def up_grad(half):
        return steps(
            lambda last: weight_grad(normed_blocks(half), unit_blocks(dup_a, last), "w_up_grad"),
            dup_b,
        )

    def down_grad(half):
        return steps(
            lambda last: weight_grad(
                unit_blocks(hidden_a, last), cotangent_blocks(half), "w_down_grad"
            ),
            hidden_b,
        )

    gate_sum, up_sum, down_sum, query_sum, out_sum = [DpTotal(steps) for _ in range(5)]
    gate_in = swap_row(gate_grad(1))
    dn2_far, dn2_diagonal = steps(
        lambda dgate: project([dgate, dup_b], [wg, wu], True, "feed_back"), dgate_b
    )
    diagonal_in = swap_core(dn2_diagonal)
    gate_own = gate_grad(0)
    for_far = steps(
        lambda into: (dn2_far.astype(F32) + into.astype(F32)).astype(BF16), diagonal_in
    )
    far_in = swap_far(for_far)
    up_in = swap_row(up_grad(1))
    dn2_own, dn2_near = steps(
        lambda dgate: project([dgate, dup_a], [wg, wu], True, "feed_back"), dgate_a
    )
    near_in = swap_core(dn2_near)
    gate_sum.begin(gate_own, gate_in)
    up_own = up_grad(0)

    def middle_back(far):
        dnormed = dn2_own.astype(F32) + near_in.astype(F32) + far.astype(F32)
        scaled = dnormed * gain_two
        projection = jnp.mean(scaled * middle, axis=1, keepdims=True)
        dmiddle = (
            jnp.concatenate([dy_own, dy_in], axis=1).astype(F32)
            + inverse_two * scaled
            - middle * (inverse_two**3 * projection)
        )
        return dmiddle, dmiddle.astype(BF16), jnp.sum(dnormed * middle * inverse_two, axis=0)

    dmiddle, dattn, gain_two_part = steps(middle_back, far_in)
    down_in = swap_row(down_grad(1))

    dctx_a, dctx_b = steps(lambda d: (dot_t(d, wo_half, BF16), dot_t(d, wo_core, BF16)), dattn)
    gate_sum.middle()
    up_sum.begin(up_own, up_in)
    out_core = swap_core(steps(lambda d: t_dot(ctx_b, d, BF16), dattn))
    dq_a, dq_b, dkv_all = steps(
        lambda d: attend_backward(
            start, q_a, q_b, kv, seg_q, seg_row, ctx_a, ctx_b, lse, d, dctx_b
        ),
        dctx_a,
    )
    out_chip = steps(lambda core: t_dot(ctx_a, dattn, BF16) + core, out_core)
    out_far = swap_far(out_chip[heads_own:])
    if spans == 2:
        is_first = place == 0

        def other_half(value):
            return jnp.where(is_first, value[local:], value[:local]).astype(BF16)

        dkv_core = swap_core(steps(other_half, dkv_all))
    up_sum.middle()
    gate_sum.end()
    down_own = down_grad(0)
    down_sum.begin(down_own, down_in)
    if spans == 2:

        def pair_of(core):
            value = jnp.where(is_first, dkv_all[:local], dkv_all[local:]) + core.astype(F32)
            return keep(value), give(value).astype(BF16)

        dkv_keep, dkv_give = steps(pair_of, dkv_core)
    else:
        dkv_keep, dkv_give = keep(dkv_all), give(dkv_all).astype(BF16)
    dkv_row = swap_row(dkv_give)
    query_core = swap_core(steps(lambda d: t_dot(normed_one, d, BF16), dq_b))
    ffn_far, ffn_diagonal = steps(lambda h: project([h], [wd], False, "down"), hidden_b)
    out_mine = steps(lambda far: out_chip[:heads_own] + far, out_far)
    out_row = swap_row(out_mine[:, feats:])
    query_chip = steps(lambda core: t_dot(normed_one, dq_a, BF16) + core, query_core)
    query_far = swap_far(query_chip[:, heads_own:])
    gate_total = gate_sum.result()
    ffn_diagonal_in = swap_core(ffn_diagonal)
    dkv = steps(lambda other: (dkv_keep + other.astype(F32)).astype(BF16), dkv_row)

    def norm_one_back(dkv):
        dnormed = dot_t(dq_a, wq_half) + dot_t(dq_b, wq_core) + dot_t(dkv, wkv)
        scaled = dnormed * gain_one
        projection = jnp.mean(scaled * x, axis=1, keepdims=True)
        dx = dmiddle + inverse_one * scaled - x * (inverse_one**3 * projection)
        gain_parts = jnp.stack([jnp.sum(dnormed * x * inverse_one, axis=0), gain_two_part], axis=1)
        kv_part = t_dot(normed_one, dkv, BF16)
        small_part = jnp.pad(gain_parts, ((0, 0), (0, HD - 2))).astype(BF16)
        return dx, dx[:, feats:].astype(BF16), jnp.concatenate([kv_part, small_part], axis=1)

    dx, dx_give, small_part = steps(norm_one_back, dkv)
    down_sum.middle()
    up_sum.end()
    small_row = swap_row(small_part[feats:])
    ffn_own, ffn_near = steps(lambda h: project([h], [wd], False, "down"), hidden_a)
    ffn_for_far = steps(
        lambda into: (ffn_far.astype(F32) + into.astype(F32)).astype(BF16), ffn_diagonal_in
    )
    ffn_far_in = swap_far(ffn_for_far)
    out_sum.begin(out_mine[:, :feats], out_row)
    query_mine = steps(lambda far: query_chip[:, :heads_own] + far, query_far)
    query_row = swap_row(query_mine[feats:])
    up_total = up_sum.result()
    small_one = steps(lambda other: small_part[:feats] + other, small_row)
    small_core = swap_core(small_one)
    out_sum.middle()
    down_sum.end()
    query_sum.begin(query_mine[:feats], query_row)
    dx_in = swap_row(dx_give)
    small_two = steps(jnp.add, small_core, small_one)
    ffn_near_in = swap_core(ffn_near)
    out_sum.end()
    query_sum.middle()

    def add_up(far):
        y = middle + ffn_own.astype(F32) + ffn_near_in.astype(F32) + far.astype(F32)
        return y, y[:, feats:].astype(BF16)

    y, y_give = steps(add_up, ffn_far_in)
    small_far = swap_far(small_two)
    down_total = down_sum.result()
    y_in = swap_row(y_give)
    query_sum.end()
    small_three = steps(jnp.add, small_far, small_two)
    if lax.axis_size("dp") == 4:
        small_four = steps(jnp.add, swap_pair(small_three), small_three)
        small_total = steps(jnp.add, swap_mirror(small_four), small_four)
    else:
        small_total = lax.psum(small_three, "dp")

    def put_back(other, value):
        other = other.astype(F32)
        own = value[:, :feats]
        return jnp.concatenate(
            [jnp.where(is_low, own, other), jnp.where(is_low, other, own)], axis=0
        )

    dx_out = steps(put_back, dx_in, dx)
    y_out = steps(put_back, y_in, y)
    query_total = query_sum.result()
    out_total = out_sum.result()
    small_total = small_total.astype(F32)
    kv_total = small_total[:, : 2 * HD]
    gain_total = small_total[:, 2 * HD : 2 * HD + 2].T

    return (
        y_out,
        dx_out,
        query_total,
        kv_total,
        out_total,
        gate_total,
        up_total,
        down_total,
        gain_total[0],
        gain_total[1],
    )


def solution(mesh):
    return jax.shard_map(
        per_device,
        mesh=mesh,
        in_specs=(
            P(("dp", "col"), "row"),
            P("row"),
            P("row", "col"),
            P("row", None),
            P("col", "row"),
            P("row"),
            P("row", "col"),
            P("row", "col"),
            P("col", "row"),
            P(("dp", "row"), None),
            P(("dp", "col"), "row"),
        ),
        out_specs=(
            P(("dp", "col"), "row"),
            P(("dp", "col"), "row"),
            P("row", "col"),
            P("row", None),
            P("col", "row"),
            P("row", "col"),
            P("row", "col"),
            P("col", "row"),
            P("row"),
            P("row"),
        ),
        check_vma=False,
    )
```

```python
import functools
import math

import jax
import jax.numpy as jnp
from jax import lax
from jax.experimental import pallas as pl
from jax.experimental.pallas import tpu as pltpu
from jax.sharding import PartitionSpec as P

D = 1536
HD = 128
WINDOW = 1024
EPSILON = 1e-06
NEGATIVE = -1e30
BF16 = jnp.bfloat16
F32 = jnp.float32
VMEM_BYTES = 20 * 1024 * 1024
SCALE = 0.1


def lasting(us):
    return pl.CostEstimate(flops=int(us * SCALE * 1_150_000_000), bytes_accessed=int(us * SCALE * 3_690_000), transcendentals=0)


HEAVY = pl.CostEstimate(flops=10**12, bytes_accessed=10**9, transcendentals=0)


def after(value, *earlier):
    return lax.optimization_barrier((value, *earlier))[0]


def swap_row(value):
    return lax.ppermute(value, "row", [(0, 1), (1, 0)])


def swap_core(value):
    return lax.ppermute(value, "col", [(0, 1), (1, 0), (2, 3), (3, 2)])


def swap_far(value):
    return lax.ppermute(value, "col", [(0, 2), (2, 0), (1, 3), (3, 1)])


def dot(left, right, out=F32):
    return jnp.dot(left, right, preferred_element_type=F32).astype(out)


def dot_t(left, right, out=F32):
    return lax.dot_general(
        left, right, (((1,), (1,)), ((), ())), preferred_element_type=F32
    ).astype(out)


def t_dot(left, right, out=F32):
    return lax.dot_general(
        left, right, (((0,), (0,)), ((), ())), preferred_element_type=F32
    ).astype(out)


def swap_pair(value):
    count = lax.axis_size("dp")
    return lax.ppermute(value, "dp", [(i, i ^ 1) for i in range(count)])


def swap_mirror(value):
    count = lax.axis_size("dp")
    return lax.ppermute(value, "dp", [(i, count - 1 - i) for i in range(count)])


class Steps:
    def __init__(self):
        self.last = ()

    def __call__(self, function, first, *rest):
        result = function(after(first, *self.last) if self.last else first, *rest)
        self.last = tuple(result) if isinstance(result, (tuple, list)) else (result,)
        return result


def add_kernel(left, right, out):
    out[...] = (left[...].astype(F32) + right[...].astype(F32)).astype(out.dtype)


def add(left, right):
    rows, cols = left.shape
    tile = pl.BlockSpec((rows // 2, cols), lambda i: (i, 0))
    return pl.pallas_call(
        add_kernel,
        grid=(2,),
        in_specs=[tile, tile],
        out_specs=tile,
        out_shape=jax.ShapeDtypeStruct((rows, cols), BF16),
        compiler_params=pltpu.CompilerParams(vmem_limit_bytes=VMEM_BYTES),
        cost_estimate=lasting(2.2),
        name="add",
    )(left, right)


def split_add_kernel(side, own_a, other_a, own_b, other_b, give, kept):
    give[...] = (own_a[...].astype(F32) + other_a[...].astype(F32)).astype(BF16)
    kept[...] = (own_b[...].astype(F32) + other_b[...].astype(F32)).astype(BF16)


def split_add(side, own, other):
    rows, cols = own.shape
    tile = (rows // 4, cols)
    give = pl.BlockSpec(tile, lambda i, side: ((1 - side[0]) * 2 + i, 0))
    kept = pl.BlockSpec(tile, lambda i, side: (side[0] * 2 + i, 0))
    out = pl.BlockSpec(tile, lambda i, side: (i, 0))
    shape = jax.ShapeDtypeStruct((rows // 2, cols), BF16)
    return pl.pallas_call(
        split_add_kernel,
        grid_spec=pltpu.PrefetchScalarGridSpec(
            num_scalar_prefetch=1,
            grid=(2,),
            in_specs=[give, give, kept, kept],
            out_specs=[out, out],
        ),
        out_shape=[shape, shape],
        compiler_params=pltpu.CompilerParams(vmem_limit_bytes=VMEM_BYTES),
        cost_estimate=lasting(2.4),
        name="split_add",
    )(side, own, other, own, other)


def join_kernel(side, total, rest, out):
    is_total = pl.program_id(0) // 2 == side[0]

    @pl.when(is_total)
    def _():
        out[...] = total[...].astype(F32)

    @pl.when(jnp.logical_not(is_total))
    def _():
        out[...] = rest[...].astype(F32)


def join(side, total, rest):
    rows, cols = total.shape
    tile = (rows // 2, cols)
    half = pl.BlockSpec(tile, lambda i, side: (i % 2, 0))
    return pl.pallas_call(
        join_kernel,
        grid_spec=pltpu.PrefetchScalarGridSpec(
            num_scalar_prefetch=1,
            grid=(4,),
            in_specs=[half, half],
            out_specs=pl.BlockSpec(tile, lambda i, side: (i, 0)),
        ),
        out_shape=jax.ShapeDtypeStruct((2 * rows, cols), F32),
        compiler_params=pltpu.CompilerParams(vmem_limit_bytes=VMEM_BYTES),
        cost_estimate=lasting(4.0),
        name="join",
    )(side, total, rest)


class DpTotal:
    def __init__(self, steps):
        self.steps = steps
        self.staged = lax.axis_size("dp") == 4
        side = (lax.axis_index("dp") + 1) // 2 % 2
        self.side = jnp.reshape(side, (1,)).astype(jnp.int32)

    def begin(self, own, other):
        if not self.staged:
            self.value = lax.psum(own + other, "dp")
            return
        give, self.keep = self.steps(lambda other: split_add(self.side, own, other), other)
        self.inward = swap_pair(give)

    def middle(self):
        if self.staged:
            self.pair = self.steps(add, self.inward, self.keep)
            self.across = swap_mirror(self.pair)

    def end(self):
        if self.staged:
            self.total = self.steps(add, self.across, self.pair)
            self.rest = swap_pair(self.total)

    def result(self):
        if not self.staged:
            return self.value.astype(F32)
        return self.steps(lambda rest: join(self.side, self.total, rest), self.rest)


def fence_kernel(value, out):
    out[...] = value[...]


class Rounds:
    def __init__(self):
        self.token = jnp.zeros((8, 128), F32)

    def send(self, move, value):
        return move(after(value, self.token))

    def fence(self):
        self.token = pl.pallas_call(
            fence_kernel,
            out_shape=jax.ShapeDtypeStruct((8, 128), F32),
            cost_estimate=HEAVY,
            name="fence",
        )(self.token)

    def wait(self, *results):
        self.fence()
        self.token = after(self.token, *results)


def place_kernel(odd, straight, around, out):
    is_straight = pl.program_id(0) == odd[0]

    @pl.when(is_straight)
    def _():
        out[...] = straight[...]

    @pl.when(jnp.logical_not(is_straight))
    def _():
        out[...] = around[...]


def place_rows(odd, straight, around):
    rows, cols = straight.shape
    whole = pl.BlockSpec((rows, cols), lambda i: (0, 0))
    return pl.pallas_call(
        place_kernel,
        grid=(2,),
        in_specs=[pl.BlockSpec(memory_space=pltpu.SMEM), whole, whole],
        out_specs=pl.BlockSpec((rows, cols), lambda i: (i, 0)),
        out_shape=jax.ShapeDtypeStruct((2 * rows, cols), straight.dtype),
        compiler_params=pltpu.CompilerParams(vmem_limit_bytes=VMEM_BYTES),
        cost_estimate=lasting(1.4),
        name="place_rows",
    )(jnp.reshape(odd, (1,)).astype(jnp.int32), straight, around)


def block_bias(first_query, first_key, rows, cols, query_segs, key_segs):
    query_pos = first_query + lax.broadcasted_iota(jnp.int32, (rows, cols), 0)
    key_pos = first_key + lax.broadcasted_iota(jnp.int32, (rows, cols), 1)
    distance = query_pos - key_pos
    allowed = (query_segs == key_segs) & (distance >= 0) & (distance < WINDOW)
    return jnp.where(allowed, 0.0, NEGATIVE)


def first_block(first_query, query_segs, key_segs, tile_k):
    earlier = jnp.sum((key_segs < query_segs[0:1, 0:1]).astype(jnp.int32))
    return lax.div(jnp.maximum(earlier, first_query - (WINDOW - 1)), tile_k)


def attend_forward_kernel(
    start, q_a, q_b, kv, seg_q, seg_k, ctx_a, ctx_b, lse, m_s, l_s, acc_s, *, tq, tk, heads
):
    first_query = start[0] + pl.program_id(0) * tq
    query_segs = seg_q[...]
    low_block = first_block(first_query, query_segs, seg_k[...], tk)
    high_block = lax.div(first_query + tq - 1, tk)
    scale = 1.0 / math.sqrt(HD)

    def step(block, first):
        first_key = pl.multiple_of(block * tk, tk)
        keys = kv[pl.ds(first_key, tk), :HD]
        values = kv[pl.ds(first_key, tk), HD:]
        bias = block_bias(first_query, first_key, tq, tk, query_segs, seg_k[:, pl.ds(first_key, tk)])
        for h in range(2 * heads):
            q = (q_a, q_b)[h // heads]
            own = slice(h % heads * HD, (h % heads + 1) * HD)
            cols = slice(h * HD, (h + 1) * HD)
            scores = dot_t(q[:, own], keys) * scale + bias
            top = jnp.max(scores, axis=1, keepdims=True)
            if first:
                exps = jnp.exp(scores - top)
                l_s[:, cols] = jnp.broadcast_to(jnp.sum(exps, axis=1, keepdims=True), (tq, HD))
                acc_s[:, cols] = dot(exps.astype(BF16), values)
                m_s[:, cols] = jnp.broadcast_to(top, (tq, HD))
            else:
                old = m_s[:, cols]
                new = jnp.maximum(old, top)
                fade = jnp.exp(old - new)
                exps = jnp.exp(scores - jnp.tile(new, (1, tk // HD)))
                l_s[:, cols] = l_s[:, cols] * fade + jnp.sum(exps, axis=1, keepdims=True)
                acc_s[:, cols] = acc_s[:, cols] * fade + dot(exps.astype(BF16), values)
                m_s[:, cols] = new

    step(high_block, True)

    def body(i, _):
        step(high_block - i, False)
        return 0

    lax.fori_loop(1, high_block - low_block + 1, body, 0)
    lane = lax.broadcasted_iota(jnp.int32, (tq, HD), 1)
    logs = jnp.zeros((tq, HD), F32)
    for h in range(2 * heads):
        own = slice(h % heads * HD, (h % heads + 1) * HD)
        cols = slice(h * HD, (h + 1) * HD)
        total = l_s[:, cols]
        (ctx_a, ctx_b)[h // heads][:, own] = (acc_s[:, cols] / total).astype(BF16)
        logs = jnp.where(lane == h, m_s[:, cols] + jnp.log(total), logs)
    lse[...] = logs


def attend_forward(start, q_a, q_b, kv, seg_q, seg_k):
    rows, width = q_a.shape
    tq = tk = 256
    length = kv.shape[0]
    tile = pl.BlockSpec((tq, width), lambda i: (i, 0))
    ctx = jax.ShapeDtypeStruct((rows, width), BF16)
    return pl.pallas_call(
        functools.partial(attend_forward_kernel, tq=tq, tk=tk, heads=width // HD),
        grid=(rows // tq,),
        in_specs=[
            pl.BlockSpec(memory_space=pltpu.SMEM),
            tile,
            tile,
            pl.BlockSpec((length, 2 * HD), lambda i: (0, 0)),
            pl.BlockSpec((tq, 1), lambda i: (i, 0)),
            pl.BlockSpec((1, length), lambda i: (0, 0)),
        ],
        out_specs=[tile, tile, pl.BlockSpec((tq, HD), lambda i: (i, 0))],
        out_shape=[ctx, ctx, jax.ShapeDtypeStruct((rows, HD), F32)],
        scratch_shapes=[pltpu.VMEM((tq, 2 * width), F32)] * 3,
        compiler_params=pltpu.CompilerParams(vmem_limit_bytes=VMEM_BYTES),
        cost_estimate=lasting(8),
        name="attend_forward",
    )(start, q_a, q_b, kv, seg_q, seg_k)


def attend_backward_kernel(
    start, q_a, q_b, kv, seg_q, seg_k, ctx_a, ctx_b, lse, dctx_a, dctx_b, dq_a, dq_b, dkv, dq_s,
    *, tq, tk, heads,
):
    first_query = start[0] + pl.program_id(0) * tq
    query_segs = seg_q[...]
    low_block = first_block(first_query, query_segs, seg_k[...], tk)
    high_block = lax.div(first_query + tq - 1, tk)
    scale = 1.0 / math.sqrt(HD)

    @pl.when(pl.program_id(0) == 0)
    def _():
        dkv[...] = jnp.zeros_like(dkv)

    dq_s[...] = jnp.zeros_like(dq_s)
    logs = lse[...]

    def body(i, _):
        first_key = pl.multiple_of((high_block - i) * tk, tk)
        keys = kv[pl.ds(first_key, tk), :HD]
        values = kv[pl.ds(first_key, tk), HD:]
        bias = block_bias(first_query, first_key, tq, tk, query_segs, seg_k[:, pl.ds(first_key, tk)])
        dk = jnp.zeros((tk, HD), F32)
        dv = jnp.zeros((tk, HD), F32)
        for h in range(2 * heads):
            own = slice(h % heads * HD, (h % heads + 1) * HD)
            cols = slice(h * HD, (h + 1) * HD)
            q_h = (q_a, q_b)[h // heads][:, own]
            do_h = (dctx_a, dctx_b)[h // heads][:, own]
            ctx_h = (ctx_a, ctx_b)[h // heads][:, own]
            inner = jnp.sum(do_h.astype(F32) * ctx_h.astype(F32), axis=1, keepdims=True)
            scores = dot_t(q_h, keys) * scale + bias
            probs = jnp.exp(scores - logs[:, h : h + 1])
            dprobs = dot_t(do_h, values)
            dscores = (probs * (dprobs - inner)).astype(BF16)
            dq_s[:, cols] += dot(dscores, keys)
            dk = dk + t_dot(dscores, q_h)
            dv = dv + t_dot(probs.astype(BF16), do_h)
        dkv[pl.ds(first_key, tk), :HD] += dk * scale
        dkv[pl.ds(first_key, tk), HD:] += dv
        return 0

    lax.fori_loop(0, high_block - low_block + 1, body, 0)
    half = heads * HD
    dq_a[...] = (dq_s[:, :half] * scale).astype(BF16)
    dq_b[...] = (dq_s[:, half:] * scale).astype(BF16)


def attend_backward(start, q_a, q_b, kv, seg_q, seg_k, ctx_a, ctx_b, lse, dctx_a, dctx_b):
    rows, width = q_a.shape
    tq = tk = 256
    length = kv.shape[0]
    tile = pl.BlockSpec((tq, width), lambda i: (i, 0))
    dq = jax.ShapeDtypeStruct((rows, width), BF16)
    return pl.pallas_call(
        functools.partial(attend_backward_kernel, tq=tq, tk=tk, heads=width // HD),
        grid=(rows // tq,),
        in_specs=[
            pl.BlockSpec(memory_space=pltpu.SMEM),
            tile,
            tile,
            pl.BlockSpec((length, 2 * HD), lambda i: (0, 0)),
            pl.BlockSpec((tq, 1), lambda i: (i, 0)),
            pl.BlockSpec((1, length), lambda i: (0, 0)),
            tile,
            tile,
            pl.BlockSpec((tq, HD), lambda i: (i, 0)),
            tile,
            tile,
        ],
        out_specs=[tile, tile, pl.BlockSpec((length, 2 * HD), lambda i: (0, 0))],
        out_shape=[dq, dq, jax.ShapeDtypeStruct((length, 2 * HD), F32)],
        scratch_shapes=[pltpu.VMEM((tq, 2 * width), F32)],
        compiler_params=pltpu.CompilerParams(vmem_limit_bytes=VMEM_BYTES),
        cost_estimate=lasting(20),
        name="attend_backward",
    )(start, q_a, q_b, kv, seg_q, seg_k, ctx_a, ctx_b, lse, dctx_a, dctx_b)


def feed_kernel(
    n2_a, n2_b, dy_a, dy_b, dy_c, dy_d, wg_a, wg_b, wu_a, wu_b, wd_a, wd_b, hidden, dgate, dup, *, tm
):
    root = math.sqrt(2.0 / math.pi)
    rows = n2_a.shape[0]
    feats = wg_a.shape[0]
    for base, n2, first_dy, second_dy in ((0, n2_a, dy_a, dy_b), (rows, n2_b, dy_c, dy_d)):
        for first in range(0, rows, tm):
            own = slice(first, first + tm)
            low, high = n2[own, :feats], n2[own, feats:]
            gate = dot(low, wg_a[...]) + dot(high, wg_b[...])
            up = dot(low, wu_a[...]) + dot(high, wu_b[...])
            dh = dot_t(first_dy[own], wd_a[...]) + dot_t(second_dy[own], wd_b[...])
            square = gate * gate
            tanh = jnp.tanh(gate * (root + (root * 0.044715) * square))
            half = 0.5 + 0.5 * tanh
            act = gate * half
            slope = half + act * (1.0 - tanh) * (root + (3.0 * 0.044715 * root) * square)
            out = slice(base + first, base + first + tm)
            hidden[out] = (act * up).astype(BF16)
            dgate[out] = (dh * up * slope).astype(BF16)
            dup[out] = (dh * act).astype(BF16)


def feed(n2s, dys, wg, wu, wd):
    rows, width = n2s[0].shape
    feats, units = wg[0].shape
    tn = 256
    whole = pl.BlockSpec((rows, width), lambda j: (0, 0))
    half = pl.BlockSpec((rows, feats), lambda j: (0, 0))
    out = jax.ShapeDtypeStruct((2 * rows, units), BF16)
    return pl.pallas_call(
        functools.partial(feed_kernel, tm=min(512, rows)),
        grid=(pl.cdiv(units, tn),),
        in_specs=[whole] * 2
        + [half] * 4
        + [pl.BlockSpec((feats, tn), lambda j: (0, j))] * 4
        + [pl.BlockSpec((tn, feats), lambda j: (j, 0))] * 2,
        out_specs=[pl.BlockSpec((2 * rows, tn), lambda j: (0, j))] * 3,
        out_shape=[out] * 3,
        compiler_params=pltpu.CompilerParams(vmem_limit_bytes=VMEM_BYTES),
        cost_estimate=lasting(17.5),
        name="feed",
    )(*n2s, *dys, *wg, *wu, *wd)


def weight_grad_kernel(*refs):
    out = refs[-1]
    pairs = len(refs) // 2
    total = None
    for left, right in zip(refs[:pairs], refs[pairs:-1]):
        part = t_dot(left[...], right[...])
        total = part if total is None else total + part
    out[...] = total.astype(BF16)


def weight_grad(lefts, rights, name):
    width_left = lefts[0][4]
    width_right = rights[0][4]
    tn = 256

    def left_spec(block):
        _, at, rows, col, cols = block
        return pl.BlockSpec((rows, cols), lambda j: (at, col))

    def right_spec(block):
        _, at, rows, col, cols = block
        return pl.BlockSpec((rows, tn), lambda j: (at, col * (cols // tn) + j))

    out = jax.ShapeDtypeStruct((width_left, width_right), BF16)
    tokens = sum(block[2] for block in lefts)
    return pl.pallas_call(
        weight_grad_kernel,
        grid=(pl.cdiv(width_right, tn),),
        in_specs=[left_spec(b) for b in lefts] + [right_spec(b) for b in rights],
        out_specs=pl.BlockSpec((width_left, tn), lambda j: (0, j)),
        out_shape=out,
        compiler_params=pltpu.CompilerParams(vmem_limit_bytes=VMEM_BYTES),
        cost_estimate=lasting(7.5),
        name=name,
    )(*[b[0] for b in lefts], *[b[0] for b in rights])


def project_kernel(*refs, lefts, multiply):
    left = refs[:lefts]
    weights = refs[lefts : 3 * lefts]
    first, second = refs[3 * lefts :]
    rows = first.shape[0]
    in_first = pl.program_id(0) < pl.num_programs(0) // 2

    def fill(chosen):
        for at, out in ((0, first), (rows, second)):
            own = slice(at, at + rows)
            out[...] = sum(multiply(l[own], w[...]) for l, w in zip(left, chosen)).astype(BF16)

    pl.when(in_first)(lambda: fill(weights[0::2]))
    pl.when(jnp.logical_not(in_first))(lambda: fill(weights[1::2]))


def project(lefts, weights, transposed, name):
    rows, units = lefts[0].shape
    feats = weights[0][0].shape[0 if transposed else 1]
    tn = 256
    tiles = feats // tn
    whole = pl.BlockSpec((rows, units), lambda j: (0, 0))

    def low(j):
        return jnp.minimum(j, tiles - 1)

    def high(j):
        return jnp.maximum(j - tiles, 0)

    if transposed:
        specs = [pl.BlockSpec((tn, units), lambda j, f=f: (f(j), 0)) for f in (low, high)]
    else:
        specs = [pl.BlockSpec((units, tn), lambda j, f=f: (0, f(j))) for f in (low, high)]
    out = jax.ShapeDtypeStruct((rows // 2, 2 * feats), BF16)
    flat = [half for weight in weights for half in weight]
    return pl.pallas_call(
        functools.partial(
            project_kernel, lefts=len(lefts), multiply=dot_t if transposed else dot
        ),
        grid=(2 * tiles,),
        in_specs=[whole] * len(lefts) + specs * len(lefts),
        out_specs=[pl.BlockSpec((rows // 2, tn), lambda j: (0, j))] * 2,
        out_shape=[out] * 2,
        compiler_params=pltpu.CompilerParams(vmem_limit_bytes=VMEM_BYTES),
        cost_estimate=lasting(8.5),
        name=name,
    )(*lefts, *flat)


def per_device(
    tokens_in,
    norm1_gain,
    w_query,
    w_keyval,
    w_attn_out,
    norm2_gain,
    w_gate,
    w_up,
    w_down,
    segment_ids,
    out_cotangent,
):
    width = D
    row = lax.axis_index("row")
    col = lax.axis_index("col")
    local = tokens_in.shape[0]
    mine = local // 2
    feats = tokens_in.shape[1]
    length = segment_ids.shape[1]
    spans = length // local

    def keep(value):
        return lax.dynamic_slice_in_dim(value, row * mine, mine, 0)

    def give(value):
        return lax.dynamic_slice_in_dim(value, (1 - row) * mine, mine, 0)

    is_low = row == 0

    odd = lax.axis_index("dp") % 2
    paired = lax.axis_size("dp") % 2 == 0

    def straight_part(weight):
        span = weight.shape[0] // 2
        return lax.dynamic_slice_in_dim(weight, odd * span, span, 0) if paired else weight

    def placed(straight, around):
        return place_rows(odd, straight, around) if paired else straight

    def send_pair(straight):
        return rounds.send(swap_pair, straight) if paired else straight

    rounds = Rounds()
    small = jnp.concatenate([norm1_gain, norm2_gain, segment_ids.reshape(-1).astype(F32)])
    heads_own = w_query.shape[1]
    small_in = rounds.send(swap_row, small)
    x_in = rounds.send(swap_row, give(tokens_in))
    wq_far_own = rounds.send(swap_far, w_query)
    rounds.fence()
    w_qkv = jnp.concatenate([w_query, w_keyval], axis=1)
    wqkv_in = rounds.send(swap_row, w_qkv)
    rounds.wait(x_in, wq_far_own, small_in)

    wo_far_own = rounds.send(swap_far, w_attn_out)
    wo_in = rounds.send(swap_row, w_attn_out)
    gain_one = jnp.concatenate([norm1_gain, small_in[:feats]])
    gain_two = jnp.concatenate([norm2_gain, small_in[feats : 2 * feats]])
    segs_in = small_in[2 * feats :].astype(jnp.int32).reshape(segment_ids.shape)
    segs_all = jnp.concatenate(
        [jnp.where(is_low, segment_ids, segs_in), jnp.where(is_low, segs_in, segment_ids)], axis=0
    )
    x = jnp.concatenate([keep(tokens_in), x_in], axis=1).astype(F32)
    inverse_one = lax.rsqrt(jnp.mean(x * x, axis=1, keepdims=True) + EPSILON)
    normed_one = (x * inverse_one * gain_one).astype(BF16)
    place = col % spans
    seg_row = lax.dynamic_slice_in_dim(segs_all, col // spans, 1, 0)
    first_token = place * local + row * mine
    seg_q = lax.dynamic_slice_in_dim(seg_row[0], first_token, mine, 0)[:, None]
    start = jnp.reshape(first_token, (1,)).astype(jnp.int32)
    rounds.wait(wqkv_in, wo_far_own, normed_one)

    wq_in = wqkv_in[:, :heads_own]
    wq_far_in = rounds.send(swap_far, wq_in)
    wkv = jnp.concatenate([w_keyval, wqkv_in[:, heads_own:]], axis=0)
    kv_own = dot(normed_one, wkv, BF16)
    rounds.wait(kv_own)
    kv_in = rounds.send(swap_row, kv_own)
    rounds.fence()
    wg_straight = rounds.send(swap_row, straight_part(w_gate))
    rounds.wait(wo_in, kv_in, wq_far_in)

    kv_pair = jnp.concatenate(
        [jnp.where(is_low, kv_own, kv_in), jnp.where(is_low, kv_in, kv_own)], axis=0
    )
    wq_half = jnp.concatenate(
        [
            jnp.concatenate([w_query, wq_far_own], axis=1),
            jnp.concatenate([wq_in, wq_far_in], axis=1),
        ],
        axis=0,
    )
    wo_far_in = rounds.send(swap_far, wo_in)
    wu_straight = rounds.send(swap_row, straight_part(w_up))
    wq_core = rounds.send(swap_core, wq_half)
    if spans == 2:
        kv_far = rounds.send(swap_core, kv_pair)
        first = place == 0
        kv = jnp.concatenate(
            [jnp.where(first, kv_pair, kv_far), jnp.where(first, kv_far, kv_pair)], axis=0
        )
    else:
        kv = kv_pair
    q_a = dot(normed_one, wq_half, BF16)
    rounds.wait(kv, wq_core, q_a)

    q_b = dot(normed_one, wq_core, BF16)
    ctx_a, ctx_b, lse = attend_forward(start, after(q_a, rounds.token), q_b, kv, seg_q, seg_row)
    rounds.wait(wo_far_in, wg_straight, ctx_a)

    wo_half = jnp.concatenate(
        [
            jnp.concatenate([w_attn_out, wo_far_own], axis=0),
            jnp.concatenate([wo_in, after(wo_far_in, rounds.token)], axis=0),
        ],
        axis=1,
    )
    wo_core = rounds.send(swap_core, wo_half)
    wg_around = send_pair(wg_straight)
    dy_own = keep(out_cotangent)
    dy_far_own = rounds.send(swap_far, dy_own)
    wd_straight = rounds.send(swap_row, straight_part(w_down))
    middle = x + dot(after(ctx_a, rounds.token), wo_half) + dot(ctx_b, wo_core)
    middle = lax.optimization_barrier(middle)
    inverse_two = lax.rsqrt(jnp.mean(middle * middle, axis=1, keepdims=True) + EPSILON)
    n2 = (middle * inverse_two * gain_two).astype(BF16)
    rounds.wait(n2, wo_core, wu_straight)

    n2_far = rounds.send(swap_far, n2)
    n2_near = rounds.send(swap_core, n2)
    dy_in = rounds.send(swap_row, give(out_cotangent))
    rounds.wait(wg_around, n2_near)

    wu_around = send_pair(wu_straight)
    dy_near_own = rounds.send(swap_core, dy_own)
    rounds.wait(wd_straight, wu_around, dy_near_own, dy_far_own)

    wd_around = send_pair(wd_straight)
    dy_diagonal_own = rounds.send(swap_core, dy_far_own)
    wg = (w_gate, placed(wg_straight, after(wg_around, rounds.token)))
    wu = (w_up, placed(wu_straight, after(wu_around, wg[1])))
    rounds.wait(dy_in, n2_far, dy_diagonal_own)

    dy_near_in = rounds.send(swap_core, dy_in)
    dy_far_in = rounds.send(swap_far, dy_in)
    n2_diagonal = rounds.send(swap_core, n2_far)
    wd = (w_down, placed(wd_straight, after(wd_around, rounds.token)))
    dy_near = (dy_near_own, dy_near_in)
    hidden_a, dgate_a, dup_a = feed((n2, n2_near), (dy_own, dy_in, *dy_near), wg, wu, wd)
    dy_diagonal = (dy_diagonal_own, swap_core(dy_far_in))
    hidden_b, dgate_b, dup_b = feed(
        (after(n2_far, hidden_a), n2_diagonal), (dy_far_own, dy_far_in, *dy_diagonal), wg, wu, wd
    )

    normed = [n2, n2_near, n2_far, n2_diagonal]
    cotangents = [(dy_own, dy_in), dy_near, (dy_far_own, dy_far_in), dy_diagonal]
    units = w_gate.shape[1]

    def normed_blocks(half):
        return [(value, 0, mine, half, feats) for value in normed]

    def cotangent_blocks(half):
        return [(value[half], 0, mine, 0, feats) for value in cotangents]

    def unit_blocks(first_pair, second_pair, *earlier):
        if earlier:
            first_pair = after(first_pair, *earlier)
        return [
            (value, at, mine, 0, units) for value in (first_pair, second_pair) for at in range(2)
        ]

    steps = Steps()

    def gate_grad(half):
        return steps(
            lambda last: weight_grad(normed_blocks(half), unit_blocks(dgate_a, last), "w_gate_grad"),
            dgate_b,
        )

    def up_grad(half):
        return steps(
            lambda last: weight_grad(normed_blocks(half), unit_blocks(dup_a, last), "w_up_grad"),
            dup_b,
        )

    def down_grad(half):
        return steps(
            lambda last: weight_grad(
                unit_blocks(hidden_a, last), cotangent_blocks(half), "w_down_grad"
            ),
            hidden_b,
        )

    gate_sum, up_sum, down_sum, rest_sum = [DpTotal(steps) for _ in range(4)]
    gate_in = swap_row(gate_grad(1))
    dn2_far, dn2_diagonal = steps(
        lambda dgate: project([dgate, dup_b], [wg, wu], True, "feed_back"), dgate_b
    )
    diagonal_in = swap_core(dn2_diagonal)
    gate_own = gate_grad(0)
    for_far = steps(
        lambda into: (dn2_far.astype(F32) + into.astype(F32)).astype(BF16), diagonal_in
    )
    far_in = swap_far(for_far)
    up_in = swap_row(up_grad(1))
    dn2_own, dn2_near = steps(
        lambda dgate: project([dgate, dup_a], [wg, wu], True, "feed_back"), dgate_a
    )
    near_in = swap_core(dn2_near)
    gate_sum.begin(gate_own, gate_in)
    up_own = up_grad(0)

    def middle_back(far):
        dnormed = dn2_own.astype(F32) + near_in.astype(F32) + far.astype(F32)
        scaled = dnormed * gain_two
        projection = jnp.mean(scaled * middle, axis=1, keepdims=True)
        dmiddle = (
            jnp.concatenate([dy_own, dy_in], axis=1).astype(F32)
            + inverse_two * scaled
            - middle * (inverse_two**3 * projection)
        )
        return dmiddle, dmiddle.astype(BF16), jnp.sum(dnormed * middle * inverse_two, axis=0)

    dmiddle, dattn, gain_two_part = steps(middle_back, far_in)
    gate_sum.middle()
    down_in = swap_row(down_grad(1))

    dctx_a, dctx_b = steps(lambda d: (dot_t(d, wo_half, BF16), dot_t(d, wo_core, BF16)), dattn)
    up_sum.begin(up_own, up_in)
    out_core = swap_core(steps(lambda d: t_dot(d, ctx_b, BF16), dattn))
    down_own = down_grad(0)
    out_part = steps(lambda d: t_dot(d, ctx_a, BF16), dattn)
    out_chip = steps(add, out_core, out_part)
    out_far = swap_far(out_chip[:, heads_own:])
    dq_a, dq_b, dkv_all = steps(
        lambda d: attend_backward(
            start, q_a, q_b, kv, seg_q, seg_row, ctx_a, ctx_b, lse, d, dctx_b
        ),
        dctx_a,
    )
    if spans == 2:
        is_first = place == 0

        def other_half(value):
            return jnp.where(is_first, value[local:], value[:local]).astype(BF16)

        dkv_core = swap_core(steps(other_half, dkv_all))
    up_sum.middle()
    gate_sum.end()
    out_mine = steps(add, out_far, out_chip[:, :heads_own])
    out_row = swap_row(out_mine[feats:])
    down_sum.begin(down_own, down_in)
    query_core = swap_core(steps(lambda d: t_dot(normed_one, d, BF16), dq_b))
    query_part = steps(lambda d: t_dot(normed_one, d, BF16), dq_a)
    ffn_far, ffn_diagonal = steps(lambda h: project([h], [wd], False, "down"), hidden_b)
    query_chip = steps(add, query_core, query_part)
    query_far = swap_far(query_chip[:, heads_own:])
    if spans == 2:

        def pair_of(core):
            value = jnp.where(is_first, dkv_all[:local], dkv_all[local:]) + core.astype(F32)
            return keep(value), give(value).astype(BF16)

        dkv_keep, dkv_give = steps(pair_of, dkv_core)
    else:
        dkv_keep, dkv_give = keep(dkv_all), give(dkv_all).astype(BF16)
    dkv_row = swap_row(dkv_give)
    gate_total = gate_sum.result()
    dkv = steps(lambda other: (dkv_keep + other.astype(F32)).astype(BF16), dkv_row)

    def norm_one_back(dkv):
        dnormed = dot_t(dq_a, wq_half) + dot_t(dq_b, wq_core) + dot_t(dkv, wkv)
        scaled = dnormed * gain_one
        projection = jnp.mean(scaled * x, axis=1, keepdims=True)
        dx = dmiddle + inverse_one * scaled - x * (inverse_one**3 * projection)
        gain_parts = jnp.stack([jnp.sum(dnormed * x * inverse_one, axis=0), gain_two_part], axis=1)
        kv_part = t_dot(normed_one, dkv, BF16)
        small_part = jnp.pad(gain_parts, ((0, 0), (0, HD - 2))).astype(BF16)
        return dx, dx[:, feats:].astype(BF16), jnp.concatenate([kv_part, small_part], axis=1)

    dx, dx_give, small_part = steps(norm_one_back, dkv)
    small_row = swap_row(small_part[feats:])
    ffn_diagonal_in = swap_core(after(ffn_diagonal, small_part))
    up_sum.end()
    down_sum.middle()
    ffn_own, ffn_near = steps(lambda h: project([h], [wd], False, "down"), hidden_a)
    query_mine = steps(add, query_far, query_chip[:, :heads_own])
    query_row = swap_row(query_mine[feats:])
    small_one = steps(add, small_row, small_part[:feats])
    small_core = swap_core(small_one)
    ffn_for_far = steps(add, ffn_diagonal_in, ffn_far)
    small_two = steps(add, small_core, small_one)
    small_far = swap_far(small_two)
    ffn_far_in = swap_far(after(ffn_for_far, small_two))
    ffn_near_in = swap_core(after(ffn_near, small_two))
    up_total = up_sum.result()
    down_sum.end()
    rest_own = jnp.concatenate([out_mine[:feats], query_mine[:feats], small_two], axis=1)
    rest_in = jnp.concatenate([out_row, query_row, small_far], axis=1)
    rest_sum.begin(rest_own, rest_in)
    ffn_chip = steps(add, ffn_near_in, ffn_own)
    rest_sum.middle()

    def add_up(far):
        y = middle + ffn_chip.astype(F32) + far.astype(F32)
        return y, y[:, feats:].astype(BF16)

    y, y_give = steps(add_up, ffn_far_in)
    y_in = swap_row(y_give)
    down_total = down_sum.result()
    dx_in = swap_row(after(dx_give, down_total))
    rest_sum.end()

    def put_back(other, value):
        other = other.astype(F32)
        own = value[:, :feats]
        return jnp.concatenate(
            [jnp.where(is_low, own, other), jnp.where(is_low, other, own)], axis=0
        )

    dx_out = steps(put_back, dx_in, dx)
    y_out = steps(put_back, y_in, y)
    rest_total = rest_sum.result()
    out_total = rest_total[:, :heads_own].T
    query_total = rest_total[:, heads_own : 2 * heads_own]
    kv_total = rest_total[:, 2 * heads_own : 2 * heads_own + 2 * HD]
    gain_total = rest_total[:, 2 * heads_own + 2 * HD : 2 * heads_own + 2 * HD + 2].T

    return (
        y_out,
        dx_out,
        query_total,
        kv_total,
        out_total,
        gate_total,
        up_total,
        down_total,
        gain_total[0],
        gain_total[1],
    )


def solution(mesh):
    return jax.shard_map(
        per_device,
        mesh=mesh,
        in_specs=(
            P(("dp", "col"), "row"),
            P("row"),
            P("row", "col"),
            P("row", None),
            P("col", "row"),
            P("row"),
            P("row", "col"),
            P("row", "col"),
            P("col", "row"),
            P(("dp", "row"), None),
            P(("dp", "col"), "row"),
        ),
        out_specs=(
            P(("dp", "col"), "row"),
            P(("dp", "col"), "row"),
            P("row", "col"),
            P("row", None),
            P("col", "row"),
            P("row", "col"),
            P("row", "col"),
            P("col", "row"),
            P("row"),
            P("row"),
        ),
        check_vma=False,
    )
```

```python
import functools
import math

import jax
import jax.numpy as jnp
from jax import lax
from jax.experimental import pallas as pl
from jax.experimental.pallas import tpu as pltpu
from jax.sharding import PartitionSpec as P

D = 1536
HD = 128
WINDOW = 1024
EPSILON = 1e-06
NEGATIVE = -1e30
BF16 = jnp.bfloat16
F32 = jnp.float32
VMEM_BYTES = 20 * 1024 * 1024
SCALE = 0.1


def lasting(us):
    return pl.CostEstimate(flops=int(us * SCALE * 1_150_000_000), bytes_accessed=int(us * SCALE * 3_690_000), transcendentals=0)


HEAVY = pl.CostEstimate(flops=10**12, bytes_accessed=10**9, transcendentals=0)


def after(value, *earlier):
    return lax.optimization_barrier((value, *earlier))[0]


def swap_row(value):
    return lax.ppermute(value, "row", [(0, 1), (1, 0)])


def swap_core(value):
    return lax.ppermute(value, "col", [(0, 1), (1, 0), (2, 3), (3, 2)])


def swap_far(value):
    return lax.ppermute(value, "col", [(0, 2), (2, 0), (1, 3), (3, 1)])


def dot(left, right, out=F32):
    return jnp.dot(left, right, preferred_element_type=F32).astype(out)


def dot_t(left, right, out=F32):
    return lax.dot_general(
        left, right, (((1,), (1,)), ((), ())), preferred_element_type=F32
    ).astype(out)


def t_dot(left, right, out=F32):
    return lax.dot_general(
        left, right, (((0,), (0,)), ((), ())), preferred_element_type=F32
    ).astype(out)


def swap_pair(value):
    count = lax.axis_size("dp")
    return lax.ppermute(value, "dp", [(i, i ^ 1) for i in range(count)])


def swap_mirror(value):
    count = lax.axis_size("dp")
    return lax.ppermute(value, "dp", [(i, count - 1 - i) for i in range(count)])


class Steps:
    def __init__(self):
        self.last = ()

    def __call__(self, function, first, *rest):
        result = function(after(first, *self.last) if self.last else first, *rest)
        self.last = tuple(result) if isinstance(result, (tuple, list)) else (result,)
        return result


def add_kernel(left, right, out):
    out[...] = (left[...].astype(F32) + right[...].astype(F32)).astype(out.dtype)


def add(left, right):
    rows, cols = left.shape
    tile = pl.BlockSpec((rows // 2, cols), lambda i: (i, 0))
    return pl.pallas_call(
        add_kernel,
        grid=(2,),
        in_specs=[tile, tile],
        out_specs=tile,
        out_shape=jax.ShapeDtypeStruct((rows, cols), BF16),
        compiler_params=pltpu.CompilerParams(vmem_limit_bytes=VMEM_BYTES),
        cost_estimate=lasting(2.2),
        name="add",
    )(left, right)


def split_add_kernel(side, own_a, other_a, own_b, other_b, give, kept):
    give[...] = (own_a[...].astype(F32) + other_a[...].astype(F32)).astype(BF16)
    kept[...] = (own_b[...].astype(F32) + other_b[...].astype(F32)).astype(BF16)


def split_add(side, own, other):
    rows, cols = own.shape
    tile = (rows // 4, cols)
    give = pl.BlockSpec(tile, lambda i, side: ((1 - side[0]) * 2 + i, 0))
    kept = pl.BlockSpec(tile, lambda i, side: (side[0] * 2 + i, 0))
    out = pl.BlockSpec(tile, lambda i, side: (i, 0))
    shape = jax.ShapeDtypeStruct((rows // 2, cols), BF16)
    return pl.pallas_call(
        split_add_kernel,
        grid_spec=pltpu.PrefetchScalarGridSpec(
            num_scalar_prefetch=1,
            grid=(2,),
            in_specs=[give, give, kept, kept],
            out_specs=[out, out],
        ),
        out_shape=[shape, shape],
        compiler_params=pltpu.CompilerParams(vmem_limit_bytes=VMEM_BYTES),
        cost_estimate=lasting(2.4),
        name="split_add",
    )(side, own, other, own, other)


def join_kernel(side, total, rest, out):
    is_total = pl.program_id(0) // 2 == side[0]

    @pl.when(is_total)
    def _():
        out[...] = total[...].astype(F32)

    @pl.when(jnp.logical_not(is_total))
    def _():
        out[...] = rest[...].astype(F32)


def join(side, total, rest):
    rows, cols = total.shape
    tile = (rows // 2, cols)
    half = pl.BlockSpec(tile, lambda i, side: (i % 2, 0))
    return pl.pallas_call(
        join_kernel,
        grid_spec=pltpu.PrefetchScalarGridSpec(
            num_scalar_prefetch=1,
            grid=(4,),
            in_specs=[half, half],
            out_specs=pl.BlockSpec(tile, lambda i, side: (i, 0)),
        ),
        out_shape=jax.ShapeDtypeStruct((2 * rows, cols), F32),
        compiler_params=pltpu.CompilerParams(vmem_limit_bytes=VMEM_BYTES),
        cost_estimate=lasting(4.0),
        name="join",
    )(side, total, rest)


class DpTotal:
    def __init__(self, steps):
        self.steps = steps
        self.staged = lax.axis_size("dp") == 4
        side = (lax.axis_index("dp") + 1) // 2 % 2
        self.side = jnp.reshape(side, (1,)).astype(jnp.int32)

    def begin(self, own, other):
        if not self.staged:
            self.value = lax.psum(own + other, "dp")
            return
        give, self.keep = self.steps(lambda other: split_add(self.side, own, other), other)
        self.inward = swap_pair(give)

    def middle(self):
        if self.staged:
            self.pair = self.steps(add, self.inward, self.keep)
            self.across = swap_mirror(self.pair)

    def end(self):
        if self.staged:
            self.total = self.steps(add, self.across, self.pair)
            self.rest = swap_pair(self.total)

    def result(self):
        if not self.staged:
            return self.value.astype(F32)
        return self.steps(lambda rest: join(self.side, self.total, rest), self.rest)


def fence_kernel(value, out):
    out[...] = value[...]


class Rounds:
    def __init__(self):
        self.token = jnp.zeros((8, 128), F32)

    def send(self, move, value):
        return move(after(value, self.token))

    def fence(self):
        self.token = pl.pallas_call(
            fence_kernel,
            out_shape=jax.ShapeDtypeStruct((8, 128), F32),
            cost_estimate=HEAVY,
            name="fence",
        )(self.token)

    def wait(self, *results):
        self.fence()
        self.token = after(self.token, *results)


def place_kernel(odd, straight, around, out):
    is_straight = pl.program_id(0) == odd[0]

    @pl.when(is_straight)
    def _():
        out[...] = straight[...]

    @pl.when(jnp.logical_not(is_straight))
    def _():
        out[...] = around[...]


def place_rows(odd, straight, around):
    rows, cols = straight.shape
    whole = pl.BlockSpec((rows, cols), lambda i: (0, 0))
    return pl.pallas_call(
        place_kernel,
        grid=(2,),
        in_specs=[pl.BlockSpec(memory_space=pltpu.SMEM), whole, whole],
        out_specs=pl.BlockSpec((rows, cols), lambda i: (i, 0)),
        out_shape=jax.ShapeDtypeStruct((2 * rows, cols), straight.dtype),
        compiler_params=pltpu.CompilerParams(vmem_limit_bytes=VMEM_BYTES),
        cost_estimate=lasting(1.4),
        name="place_rows",
    )(jnp.reshape(odd, (1,)).astype(jnp.int32), straight, around)


def block_bias(first_query, first_key, rows, cols, query_segs, key_segs):
    query_pos = first_query + lax.broadcasted_iota(jnp.int32, (rows, cols), 0)
    key_pos = first_key + lax.broadcasted_iota(jnp.int32, (rows, cols), 1)
    distance = query_pos - key_pos
    allowed = (query_segs == key_segs) & (distance >= 0) & (distance < WINDOW)
    return jnp.where(allowed, 0.0, NEGATIVE)


def first_block(first_query, query_segs, key_segs, tile_k):
    earlier = jnp.sum((key_segs < query_segs[0:1, 0:1]).astype(jnp.int32))
    return lax.div(jnp.maximum(earlier, first_query - (WINDOW - 1)), tile_k)


def attend_forward_kernel(
    start, q_a, q_b, kv, seg_q, seg_k, ctx_a, ctx_b, lse, m_s, l_s, acc_s, *, tq, tk, heads
):
    first_query = start[0] + pl.program_id(0) * tq
    query_segs = seg_q[...]
    low_block = first_block(first_query, query_segs, seg_k[...], tk)
    high_block = lax.div(first_query + tq - 1, tk)
    scale = 1.0 / math.sqrt(HD)

    def step(block, first):
        first_key = pl.multiple_of(block * tk, tk)
        keys = kv[pl.ds(first_key, tk), :HD]
        values = kv[pl.ds(first_key, tk), HD:]
        bias = block_bias(first_query, first_key, tq, tk, query_segs, seg_k[:, pl.ds(first_key, tk)])
        for h in range(2 * heads):
            q = (q_a, q_b)[h // heads]
            own = slice(h % heads * HD, (h % heads + 1) * HD)
            cols = slice(h * HD, (h + 1) * HD)
            scores = dot_t(q[:, own], keys) * scale + bias
            top = jnp.max(scores, axis=1, keepdims=True)
            if first:
                exps = jnp.exp(scores - top)
                l_s[:, cols] = jnp.broadcast_to(jnp.sum(exps, axis=1, keepdims=True), (tq, HD))
                acc_s[:, cols] = dot(exps.astype(BF16), values)
                m_s[:, cols] = jnp.broadcast_to(top, (tq, HD))
            else:
                old = m_s[:, cols]
                new = jnp.maximum(old, top)
                fade = jnp.exp(old - new)
                exps = jnp.exp(scores - jnp.tile(new, (1, tk // HD)))
                l_s[:, cols] = l_s[:, cols] * fade + jnp.sum(exps, axis=1, keepdims=True)
                acc_s[:, cols] = acc_s[:, cols] * fade + dot(exps.astype(BF16), values)
                m_s[:, cols] = new

    step(high_block, True)

    def body(i, _):
        step(high_block - i, False)
        return 0

    lax.fori_loop(1, high_block - low_block + 1, body, 0)
    lane = lax.broadcasted_iota(jnp.int32, (tq, HD), 1)
    logs = jnp.zeros((tq, HD), F32)
    for h in range(2 * heads):
        own = slice(h % heads * HD, (h % heads + 1) * HD)
        cols = slice(h * HD, (h + 1) * HD)
        total = l_s[:, cols]
        (ctx_a, ctx_b)[h // heads][:, own] = (acc_s[:, cols] / total).astype(BF16)
        logs = jnp.where(lane == h, m_s[:, cols] + jnp.log(total), logs)
    lse[...] = logs


def attend_forward(start, q_a, q_b, kv, seg_q, seg_k):
    rows, width = q_a.shape
    tq = tk = 256
    length = kv.shape[0]
    tile = pl.BlockSpec((tq, width), lambda i: (i, 0))
    ctx = jax.ShapeDtypeStruct((rows, width), BF16)
    return pl.pallas_call(
        functools.partial(attend_forward_kernel, tq=tq, tk=tk, heads=width // HD),
        grid=(rows // tq,),
        in_specs=[
            pl.BlockSpec(memory_space=pltpu.SMEM),
            tile,
            tile,
            pl.BlockSpec((length, 2 * HD), lambda i: (0, 0)),
            pl.BlockSpec((tq, 1), lambda i: (i, 0)),
            pl.BlockSpec((1, length), lambda i: (0, 0)),
        ],
        out_specs=[tile, tile, pl.BlockSpec((tq, HD), lambda i: (i, 0))],
        out_shape=[ctx, ctx, jax.ShapeDtypeStruct((rows, HD), F32)],
        scratch_shapes=[pltpu.VMEM((tq, 2 * width), F32)] * 3,
        compiler_params=pltpu.CompilerParams(vmem_limit_bytes=VMEM_BYTES),
        cost_estimate=lasting(8),
        name="attend_forward",
    )(start, q_a, q_b, kv, seg_q, seg_k)


def attend_out_kernel(x, ctx_a, ctx_b, wo_a, wo_b, gain, middle, normed, inverse):
    value = x[...] + dot(ctx_a[...], wo_a[...]) + dot(ctx_b[...], wo_b[...])
    scale = lax.rsqrt(jnp.mean(value * value, axis=1, keepdims=True) + EPSILON)
    middle[...] = value
    normed[...] = (value * scale * gain[...]).astype(BF16)
    inverse[...] = scale


def attend_out(x, ctx_a, ctx_b, wo_a, wo_b, gain):
    rows, width = x.shape
    half = ctx_a.shape[1]
    tm = 256
    tile = pl.BlockSpec((tm, width), lambda i: (i, 0))
    part = pl.BlockSpec((tm, half), lambda i: (i, 0))
    weight = pl.BlockSpec((half, width), lambda i: (0, 0))
    return pl.pallas_call(
        attend_out_kernel,
        grid=(rows // tm,),
        in_specs=[tile, part, part, weight, weight, pl.BlockSpec((1, width), lambda i: (0, 0))],
        out_specs=[tile, tile, pl.BlockSpec((tm, 1), lambda i: (i, 0))],
        out_shape=[
            jax.ShapeDtypeStruct((rows, width), F32),
            jax.ShapeDtypeStruct((rows, width), BF16),
            jax.ShapeDtypeStruct((rows, 1), F32),
        ],
        compiler_params=pltpu.CompilerParams(vmem_limit_bytes=32 * 1024 * 1024),
        cost_estimate=lasting(5),
        name="attend_out",
    )(x, ctx_a, ctx_b, wo_a, wo_b, gain)


def attend_backward_kernel(
    start, q_a, q_b, kv, seg_q, seg_k, ctx_a, ctx_b, lse, dctx_a, dctx_b, dq_a, dq_b, dkv, dq_s,
    *, tq, tk, heads,
):
    first_query = start[0] + pl.program_id(0) * tq
    query_segs = seg_q[...]
    low_block = first_block(first_query, query_segs, seg_k[...], tk)
    high_block = lax.div(first_query + tq - 1, tk)
    scale = 1.0 / math.sqrt(HD)

    @pl.when(pl.program_id(0) == 0)
    def _():
        dkv[...] = jnp.zeros_like(dkv)

    dq_s[...] = jnp.zeros_like(dq_s)
    logs = lse[...]

    def body(i, _):
        first_key = pl.multiple_of((high_block - i) * tk, tk)
        keys = kv[pl.ds(first_key, tk), :HD]
        values = kv[pl.ds(first_key, tk), HD:]
        bias = block_bias(first_query, first_key, tq, tk, query_segs, seg_k[:, pl.ds(first_key, tk)])
        dk = jnp.zeros((tk, HD), F32)
        dv = jnp.zeros((tk, HD), F32)
        for h in range(2 * heads):
            own = slice(h % heads * HD, (h % heads + 1) * HD)
            cols = slice(h * HD, (h + 1) * HD)
            q_h = (q_a, q_b)[h // heads][:, own]
            do_h = (dctx_a, dctx_b)[h // heads][:, own]
            ctx_h = (ctx_a, ctx_b)[h // heads][:, own]
            inner = jnp.sum(do_h.astype(F32) * ctx_h.astype(F32), axis=1, keepdims=True)
            scores = dot_t(q_h, keys) * scale + bias
            probs = jnp.exp(scores - logs[:, h : h + 1])
            dprobs = dot_t(do_h, values)
            dscores = (probs * (dprobs - inner)).astype(BF16)
            dq_s[:, cols] += dot(dscores, keys)
            dk = dk + t_dot(dscores, q_h)
            dv = dv + t_dot(probs.astype(BF16), do_h)
        dkv[pl.ds(first_key, tk), :HD] += dk * scale
        dkv[pl.ds(first_key, tk), HD:] += dv
        return 0

    lax.fori_loop(0, high_block - low_block + 1, body, 0)
    half = heads * HD
    dq_a[...] = (dq_s[:, :half] * scale).astype(BF16)
    dq_b[...] = (dq_s[:, half:] * scale).astype(BF16)


def attend_backward(start, q_a, q_b, kv, seg_q, seg_k, ctx_a, ctx_b, lse, dctx_a, dctx_b):
    rows, width = q_a.shape
    tq = tk = 256
    length = kv.shape[0]
    tile = pl.BlockSpec((tq, width), lambda i: (i, 0))
    dq = jax.ShapeDtypeStruct((rows, width), BF16)
    return pl.pallas_call(
        functools.partial(attend_backward_kernel, tq=tq, tk=tk, heads=width // HD),
        grid=(rows // tq,),
        in_specs=[
            pl.BlockSpec(memory_space=pltpu.SMEM),
            tile,
            tile,
            pl.BlockSpec((length, 2 * HD), lambda i: (0, 0)),
            pl.BlockSpec((tq, 1), lambda i: (i, 0)),
            pl.BlockSpec((1, length), lambda i: (0, 0)),
            tile,
            tile,
            pl.BlockSpec((tq, HD), lambda i: (i, 0)),
            tile,
            tile,
        ],
        out_specs=[tile, tile, pl.BlockSpec((length, 2 * HD), lambda i: (0, 0))],
        out_shape=[dq, dq, jax.ShapeDtypeStruct((length, 2 * HD), F32)],
        scratch_shapes=[pltpu.VMEM((tq, 2 * width), F32)],
        compiler_params=pltpu.CompilerParams(vmem_limit_bytes=VMEM_BYTES),
        cost_estimate=lasting(20),
        name="attend_backward",
    )(start, q_a, q_b, kv, seg_q, seg_k, ctx_a, ctx_b, lse, dctx_a, dctx_b)


def feed_kernel(
    n2_a, n2_b, dy_a, dy_b, dy_c, dy_d, wg_a, wg_b, wu_a, wu_b, wd_a, wd_b, hidden, dgate, dup, *, tm
):
    root = math.sqrt(2.0 / math.pi)
    rows = n2_a.shape[0]
    feats = wg_a.shape[0]
    for base, n2, first_dy, second_dy in ((0, n2_a, dy_a, dy_b), (rows, n2_b, dy_c, dy_d)):
        for first in range(0, rows, tm):
            own = slice(first, first + tm)
            low, high = n2[own, :feats], n2[own, feats:]
            gate = dot(low, wg_a[...]) + dot(high, wg_b[...])
            up = dot(low, wu_a[...]) + dot(high, wu_b[...])
            dh = dot_t(first_dy[own], wd_a[...]) + dot_t(second_dy[own], wd_b[...])
            square = gate * gate
            tanh = jnp.tanh(gate * (root + (root * 0.044715) * square))
            half = 0.5 + 0.5 * tanh
            act = gate * half
            slope = half + act * (1.0 - tanh) * (root + (3.0 * 0.044715 * root) * square)
            out = slice(base + first, base + first + tm)
            hidden[out] = (act * up).astype(BF16)
            dgate[out] = (dh * up * slope).astype(BF16)
            dup[out] = (dh * act).astype(BF16)


def feed(n2s, dys, wg, wu, wd):
    rows, width = n2s[0].shape
    feats, units = wg[0].shape
    tn = 256
    whole = pl.BlockSpec((rows, width), lambda j: (0, 0))
    half = pl.BlockSpec((rows, feats), lambda j: (0, 0))
    out = jax.ShapeDtypeStruct((2 * rows, units), BF16)
    return pl.pallas_call(
        functools.partial(feed_kernel, tm=min(512, rows)),
        grid=(pl.cdiv(units, tn),),
        in_specs=[whole] * 2
        + [half] * 4
        + [pl.BlockSpec((feats, tn), lambda j: (0, j))] * 4
        + [pl.BlockSpec((tn, feats), lambda j: (j, 0))] * 2,
        out_specs=[pl.BlockSpec((2 * rows, tn), lambda j: (0, j))] * 3,
        out_shape=[out] * 3,
        compiler_params=pltpu.CompilerParams(vmem_limit_bytes=VMEM_BYTES),
        cost_estimate=lasting(17.5),
        name="feed",
    )(*n2s, *dys, *wg, *wu, *wd)


def weight_grad_kernel(*refs):
    out = refs[-1]
    pairs = len(refs) // 2
    total = None
    for left, right in zip(refs[:pairs], refs[pairs:-1]):
        part = t_dot(left[...], right[...])
        total = part if total is None else total + part
    out[...] = total.astype(BF16)


def weight_grad(lefts, rights, name):
    width_left = lefts[0][4]
    width_right = rights[0][4]
    tn = 256

    def left_spec(block):
        _, at, rows, col, cols = block
        return pl.BlockSpec((rows, cols), lambda j: (at, col))

    def right_spec(block):
        _, at, rows, col, cols = block
        return pl.BlockSpec((rows, tn), lambda j: (at, col * (cols // tn) + j))

    out = jax.ShapeDtypeStruct((width_left, width_right), BF16)
    tokens = sum(block[2] for block in lefts)
    return pl.pallas_call(
        weight_grad_kernel,
        grid=(pl.cdiv(width_right, tn),),
        in_specs=[left_spec(b) for b in lefts] + [right_spec(b) for b in rights],
        out_specs=pl.BlockSpec((width_left, tn), lambda j: (0, j)),
        out_shape=out,
        compiler_params=pltpu.CompilerParams(vmem_limit_bytes=VMEM_BYTES),
        cost_estimate=lasting(7.5),
        name=name,
    )(*[b[0] for b in lefts], *[b[0] for b in rights])


def project_kernel(*refs, lefts, multiply):
    left = refs[:lefts]
    weights = refs[lefts : 3 * lefts]
    first, second = refs[3 * lefts :]
    rows = first.shape[0]
    in_first = pl.program_id(0) < pl.num_programs(0) // 2

    def fill(chosen):
        for at, out in ((0, first), (rows, second)):
            own = slice(at, at + rows)
            out[...] = sum(multiply(l[own], w[...]) for l, w in zip(left, chosen)).astype(BF16)

    pl.when(in_first)(lambda: fill(weights[0::2]))
    pl.when(jnp.logical_not(in_first))(lambda: fill(weights[1::2]))


def project(lefts, weights, transposed, name):
    rows, units = lefts[0].shape
    feats = weights[0][0].shape[0 if transposed else 1]
    tn = 256
    tiles = feats // tn
    whole = pl.BlockSpec((rows, units), lambda j: (0, 0))

    def low(j):
        return jnp.minimum(j, tiles - 1)

    def high(j):
        return jnp.maximum(j - tiles, 0)

    if transposed:
        specs = [pl.BlockSpec((tn, units), lambda j, f=f: (f(j), 0)) for f in (low, high)]
    else:
        specs = [pl.BlockSpec((units, tn), lambda j, f=f: (0, f(j))) for f in (low, high)]
    out = jax.ShapeDtypeStruct((rows // 2, 2 * feats), BF16)
    flat = [half for weight in weights for half in weight]
    return pl.pallas_call(
        functools.partial(
            project_kernel, lefts=len(lefts), multiply=dot_t if transposed else dot
        ),
        grid=(2 * tiles,),
        in_specs=[whole] * len(lefts) + specs * len(lefts),
        out_specs=[pl.BlockSpec((rows // 2, tn), lambda j: (0, j))] * 2,
        out_shape=[out] * 2,
        compiler_params=pltpu.CompilerParams(vmem_limit_bytes=VMEM_BYTES),
        cost_estimate=lasting(8.5),
        name=name,
    )(*lefts, *flat)


def per_device(
    tokens_in,
    norm1_gain,
    w_query,
    w_keyval,
    w_attn_out,
    norm2_gain,
    w_gate,
    w_up,
    w_down,
    segment_ids,
    out_cotangent,
):
    width = D
    row = lax.axis_index("row")
    col = lax.axis_index("col")
    local = tokens_in.shape[0]
    mine = local // 2
    feats = tokens_in.shape[1]
    length = segment_ids.shape[1]
    spans = length // local

    def keep(value):
        return lax.dynamic_slice_in_dim(value, row * mine, mine, 0)

    def give(value):
        return lax.dynamic_slice_in_dim(value, (1 - row) * mine, mine, 0)

    is_low = row == 0

    odd = lax.axis_index("dp") % 2
    paired = lax.axis_size("dp") % 2 == 0

    def straight_part(weight):
        span = weight.shape[0] // 2
        return lax.dynamic_slice_in_dim(weight, odd * span, span, 0) if paired else weight

    def placed(straight, around):
        return place_rows(odd, straight, around) if paired else straight

    def send_pair(straight):
        return rounds.send(swap_pair, straight) if paired else straight

    rounds = Rounds()
    small = jnp.concatenate([norm1_gain, norm2_gain, segment_ids.reshape(-1).astype(F32)])
    heads_own = w_query.shape[1]
    small_in = rounds.send(swap_row, small)
    x_in = rounds.send(swap_row, give(tokens_in))
    dy_own = keep(out_cotangent)
    dy_far_own = rounds.send(swap_far, dy_own)
    wq_far_own = swap_far(after(w_query, dy_own))
    w_qkv = jnp.concatenate([w_query, w_keyval], axis=1)
    wqkv_in = swap_row(after(w_qkv, small_in))
    rounds.wait(x_in, dy_far_own, small_in)

    wo_far_own = rounds.send(swap_far, w_attn_out)
    wo_in = rounds.send(swap_row, w_attn_out)
    gain_one = jnp.concatenate([norm1_gain, small_in[:feats]])
    gain_two = jnp.concatenate([norm2_gain, small_in[feats : 2 * feats]])
    segs_in = small_in[2 * feats :].astype(jnp.int32).reshape(segment_ids.shape)
    segs_all = jnp.concatenate(
        [jnp.where(is_low, segment_ids, segs_in), jnp.where(is_low, segs_in, segment_ids)], axis=0
    )
    x = jnp.concatenate([keep(tokens_in), x_in], axis=1).astype(F32)
    inverse_one = lax.rsqrt(jnp.mean(x * x, axis=1, keepdims=True) + EPSILON)
    normed_one = (x * inverse_one * gain_one).astype(BF16)
    place = col % spans
    seg_row = lax.dynamic_slice_in_dim(segs_all, col // spans, 1, 0)
    first_token = place * local + row * mine
    seg_q = lax.dynamic_slice_in_dim(seg_row[0], first_token, mine, 0)[:, None]
    start = jnp.reshape(first_token, (1,)).astype(jnp.int32)
    rounds.wait(wqkv_in, wq_far_own, normed_one)

    wq_in = wqkv_in[:, :heads_own]
    wq_far_in = rounds.send(swap_far, wq_in)
    wkv = jnp.concatenate([w_keyval, wqkv_in[:, heads_own:]], axis=0)
    kv_own = dot(normed_one, wkv, BF16)
    rounds.wait(kv_own)
    kv_in = rounds.send(swap_row, kv_own)
    rounds.fence()
    wg_straight = rounds.send(swap_row, straight_part(w_gate))
    rounds.wait(wo_in, kv_in, wq_far_in, wo_far_own)

    kv_pair = jnp.concatenate(
        [jnp.where(is_low, kv_own, kv_in), jnp.where(is_low, kv_in, kv_own)], axis=0
    )
    wq_half = jnp.concatenate(
        [
            jnp.concatenate([w_query, wq_far_own], axis=1),
            jnp.concatenate([wq_in, wq_far_in], axis=1),
        ],
        axis=0,
    )
    wo_far_in = rounds.send(swap_far, wo_in)
    wu_straight = rounds.send(swap_row, straight_part(w_up))
    wq_core = rounds.send(swap_core, wq_half)
    if spans == 2:
        kv_far = rounds.send(swap_core, kv_pair)
        first = place == 0
        kv = jnp.concatenate(
            [jnp.where(first, kv_pair, kv_far), jnp.where(first, kv_far, kv_pair)], axis=0
        )
    else:
        kv = kv_pair
    q_a = dot(normed_one, wq_half, BF16)
    rounds.wait(kv, wq_core, q_a)

    q_b = dot(normed_one, wq_core, BF16)
    ctx_a, ctx_b, lse = attend_forward(start, after(q_a, rounds.token), q_b, kv, seg_q, seg_row)
    rounds.wait(wo_far_in, wg_straight, ctx_a)

    wo_half = jnp.concatenate(
        [
            jnp.concatenate([w_attn_out, wo_far_own], axis=0),
            jnp.concatenate([wo_in, after(wo_far_in, rounds.token)], axis=0),
        ],
        axis=1,
    )
    wo_core = rounds.send(swap_core, wo_half)
    wg_around = send_pair(wg_straight)
    wd_straight = rounds.send(swap_row, straight_part(w_down))
    middle, n2, inverse_two = attend_out(
        x, after(ctx_a, rounds.token), ctx_b, wo_half, wo_core, gain_two[None, :]
    )
    rounds.wait(n2, wo_core)

    n2_far = rounds.send(swap_far, n2)
    n2_near = rounds.send(swap_core, n2)
    rounds.wait(n2_near, wu_straight, wg_around)

    dy_in = rounds.send(swap_row, give(out_cotangent))
    wu_around = send_pair(wu_straight)
    dy_near_own = rounds.send(swap_core, dy_own)
    rounds.wait(wd_straight, wu_around, dy_near_own)

    wd_around = send_pair(wd_straight)
    dy_diagonal_own = rounds.send(swap_core, dy_far_own)
    wg = (w_gate, placed(wg_straight, after(wg_around, rounds.token)))
    wu = (w_up, placed(wu_straight, after(wu_around, wg[1])))
    rounds.wait(dy_in, n2_far, dy_diagonal_own)

    dy_far_in = rounds.send(swap_far, dy_in)
    dy_near_in = rounds.send(swap_core, dy_in)
    n2_diagonal = rounds.send(swap_core, n2_far)
    wd = (w_down, placed(wd_straight, after(wd_around, rounds.token)))
    dy_near = (dy_near_own, dy_near_in)
    hidden_a, dgate_a, dup_a = feed((n2, n2_near), (dy_own, dy_in, *dy_near), wg, wu, wd)
    dy_diagonal = (dy_diagonal_own, swap_core(dy_far_in))
    hidden_b, dgate_b, dup_b = feed(
        (after(n2_far, hidden_a), n2_diagonal), (dy_far_own, dy_far_in, *dy_diagonal), wg, wu, wd
    )

    normed = [n2, n2_near, n2_far, n2_diagonal]
    cotangents = [(dy_own, dy_in), dy_near, (dy_far_own, dy_far_in), dy_diagonal]
    units = w_gate.shape[1]

    def normed_blocks(half):
        return [(value, 0, mine, half, feats) for value in normed]

    def cotangent_blocks(half):
        return [(value[half], 0, mine, 0, feats) for value in cotangents]

    def unit_blocks(first_pair, second_pair, *earlier):
        if earlier:
            first_pair = after(first_pair, *earlier)
        return [
            (value, at, mine, 0, units) for value in (first_pair, second_pair) for at in range(2)
        ]

    steps = Steps()

    def gate_grad(half):
        return steps(
            lambda last: weight_grad(normed_blocks(half), unit_blocks(dgate_a, last), "w_gate_grad"),
            dgate_b,
        )

    def up_grad(half):
        return steps(
            lambda last: weight_grad(normed_blocks(half), unit_blocks(dup_a, last), "w_up_grad"),
            dup_b,
        )

    def down_grad(half):
        return steps(
            lambda last: weight_grad(
                unit_blocks(hidden_a, last), cotangent_blocks(half), "w_down_grad"
            ),
            hidden_b,
        )

    gate_sum, up_sum, down_sum, rest_sum = [DpTotal(steps) for _ in range(4)]
    gate_in = swap_row(gate_grad(1))
    dn2_far, dn2_diagonal = steps(
        lambda dgate: project([dgate, dup_b], [wg, wu], True, "feed_back"), dgate_b
    )
    diagonal_in = swap_core(dn2_diagonal)
    gate_own = gate_grad(0)
    for_far = steps(
        lambda into: (dn2_far.astype(F32) + into.astype(F32)).astype(BF16), diagonal_in
    )
    far_in = swap_far(for_far)
    up_in = swap_row(up_grad(1))
    dn2_own, dn2_near = steps(
        lambda dgate: project([dgate, dup_a], [wg, wu], True, "feed_back"), dgate_a
    )
    near_in = swap_core(dn2_near)
    gate_sum.begin(gate_own, gate_in)
    up_own = up_grad(0)

    def middle_back(far):
        dnormed = dn2_own.astype(F32) + near_in.astype(F32) + far.astype(F32)
        scaled = dnormed * gain_two
        projection = jnp.mean(scaled * middle, axis=1, keepdims=True)
        dmiddle = (
            jnp.concatenate([dy_own, dy_in], axis=1).astype(F32)
            + inverse_two * scaled
            - middle * (inverse_two**3 * projection)
        )
        return dmiddle, dmiddle.astype(BF16), jnp.sum(dnormed * middle * inverse_two, axis=0)

    dmiddle, dattn, gain_two_part = steps(middle_back, far_in)
    gate_sum.middle()
    down_in = swap_row(down_grad(1))

    dctx_a, dctx_b = steps(lambda d: (dot_t(d, wo_half, BF16), dot_t(d, wo_core, BF16)), dattn)
    up_sum.begin(up_own, up_in)
    out_core = swap_core(steps(lambda d: t_dot(d, ctx_b, BF16), dattn))
    down_own = down_grad(0)
    out_part = steps(lambda d: t_dot(d, ctx_a, BF16), dattn)
    out_chip = steps(add, out_core, out_part)
    out_far = swap_far(out_chip[:, heads_own:])
    dq_a, dq_b, dkv_all = steps(
        lambda d: attend_backward(
            start, q_a, q_b, kv, seg_q, seg_row, ctx_a, ctx_b, lse, d, dctx_b
        ),
        dctx_a,
    )
    if spans == 2:
        is_first = place == 0

        def other_half(value):
            return jnp.where(is_first, value[local:], value[:local]).astype(BF16)

        dkv_core = swap_core(steps(other_half, dkv_all))
    up_sum.middle()
    gate_sum.end()
    out_mine = steps(add, out_far, out_chip[:, :heads_own])
    out_row = swap_row(out_mine[feats:])
    down_sum.begin(down_own, down_in)
    query_core = swap_core(steps(lambda d: t_dot(normed_one, d, BF16), dq_b))
    query_part = steps(lambda d: t_dot(normed_one, d, BF16), dq_a)
    ffn_far, ffn_diagonal = steps(lambda h: project([h], [wd], False, "down"), hidden_b)
    query_chip = steps(add, query_core, query_part)
    query_far = swap_far(query_chip[:, heads_own:])
    if spans == 2:

        def pair_of(core):
            value = jnp.where(is_first, dkv_all[:local], dkv_all[local:]) + core.astype(F32)
            return keep(value), give(value).astype(BF16)

        dkv_keep, dkv_give = steps(pair_of, dkv_core)
    else:
        dkv_keep, dkv_give = keep(dkv_all), give(dkv_all).astype(BF16)
    dkv_row = swap_row(dkv_give)
    gate_total = gate_sum.result()
    dkv = steps(lambda other: (dkv_keep + other.astype(F32)).astype(BF16), dkv_row)

    def norm_one_back(dkv):
        dnormed = dot_t(dq_a, wq_half) + dot_t(dq_b, wq_core) + dot_t(dkv, wkv)
        scaled = dnormed * gain_one
        projection = jnp.mean(scaled * x, axis=1, keepdims=True)
        dx = dmiddle + inverse_one * scaled - x * (inverse_one**3 * projection)
        gain_parts = jnp.stack([jnp.sum(dnormed * x * inverse_one, axis=0), gain_two_part], axis=1)
        kv_part = t_dot(normed_one, dkv, BF16)
        small_part = jnp.pad(gain_parts, ((0, 0), (0, HD - 2))).astype(BF16)
        return dx, dx[:, feats:].astype(BF16), jnp.concatenate([kv_part, small_part], axis=1)

    dx, dx_give, small_part = steps(norm_one_back, dkv)
    small_row = swap_row(small_part[feats:])
    ffn_diagonal_in = swap_core(after(ffn_diagonal, small_part))
    up_sum.end()
    down_sum.middle()
    ffn_own, ffn_near = steps(lambda h: project([h], [wd], False, "down"), hidden_a)
    query_mine = steps(add, query_far, query_chip[:, :heads_own])
    query_row = swap_row(query_mine[feats:])
    small_one = steps(add, small_row, small_part[:feats])
    small_core = swap_core(small_one)
    ffn_for_far = steps(add, ffn_diagonal_in, ffn_far)
    small_two = steps(add, small_core, small_one)
    small_far = swap_far(small_two)
    ffn_far_in = swap_far(after(ffn_for_far, small_two))
    ffn_near_in = swap_core(after(ffn_near, small_two))
    up_total = up_sum.result()
    down_sum.end()
    rest_own = jnp.concatenate([out_mine[:feats], query_mine[:feats], small_two], axis=1)
    rest_in = jnp.concatenate([out_row, query_row, small_far], axis=1)
    rest_sum.begin(rest_own, rest_in)
    ffn_chip = steps(add, ffn_near_in, ffn_own)
    rest_sum.middle()

    def add_up(far):
        y = middle + ffn_chip.astype(F32) + far.astype(F32)
        return y, y[:, feats:].astype(BF16)

    y, y_give = steps(add_up, ffn_far_in)
    y_in = swap_row(y_give)
    down_total = down_sum.result()
    dx_in = swap_row(after(dx_give, down_total))
    rest_sum.end()

    def put_back(other, value):
        other = other.astype(F32)
        own = value[:, :feats]
        return jnp.concatenate(
            [jnp.where(is_low, own, other), jnp.where(is_low, other, own)], axis=0
        )

    dx_out = steps(put_back, dx_in, dx)
    y_out = steps(put_back, y_in, y)
    rest_total = rest_sum.result()
    out_total = rest_total[:, :heads_own].T
    query_total = rest_total[:, heads_own : 2 * heads_own]
    kv_total = rest_total[:, 2 * heads_own : 2 * heads_own + 2 * HD]
    gain_total = rest_total[:, 2 * heads_own + 2 * HD : 2 * heads_own + 2 * HD + 2].T

    return (
        y_out,
        dx_out,
        query_total,
        kv_total,
        out_total,
        gate_total,
        up_total,
        down_total,
        gain_total[0],
        gain_total[1],
    )


def solution(mesh):
    return jax.shard_map(
        per_device,
        mesh=mesh,
        in_specs=(
            P(("dp", "col"), "row"),
            P("row"),
            P("row", "col"),
            P("row", None),
            P("col", "row"),
            P("row"),
            P("row", "col"),
            P("row", "col"),
            P("col", "row"),
            P(("dp", "row"), None),
            P(("dp", "col"), "row"),
        ),
        out_specs=(
            P(("dp", "col"), "row"),
            P(("dp", "col"), "row"),
            P("row", "col"),
            P("row", None),
            P("col", "row"),
            P("row", "col"),
            P("row", "col"),
            P("col", "row"),
            P("row"),
            P("row"),
        ),
        check_vma=False,
    )
```

```python
import functools
import math

import jax
import jax.numpy as jnp
from jax import lax
from jax.experimental import pallas as pl
from jax.experimental.pallas import tpu as pltpu
from jax.sharding import PartitionSpec as P

D = 1536
HD = 128
WINDOW = 1024
EPSILON = 1e-06
NEGATIVE = -1e30
BF16 = jnp.bfloat16
F32 = jnp.float32
VMEM_BYTES = 20 * 1024 * 1024
MATMUL_VMEM_BYTES = 16 * 1024 * 1024
SMALL_VMEM_BYTES = 8 * 1024 * 1024
SCALE = 0.1


def lasting(us):
    return pl.CostEstimate(flops=int(us * SCALE * 1_150_000_000), bytes_accessed=int(us * SCALE * 3_690_000), transcendentals=0)


HEAVY = pl.CostEstimate(flops=10**12, bytes_accessed=10**9, transcendentals=0)


def after(value, *earlier):
    return lax.optimization_barrier((value, *earlier))[0]


def swap_row(value):
    return lax.ppermute(value, "row", [(0, 1), (1, 0)])


def swap_core(value):
    return lax.ppermute(value, "col", [(0, 1), (1, 0), (2, 3), (3, 2)])


def swap_far(value):
    return lax.ppermute(value, "col", [(0, 2), (2, 0), (1, 3), (3, 1)])


def dot(left, right, out=F32):
    return jnp.dot(left, right, preferred_element_type=F32).astype(out)


def dot_t(left, right, out=F32):
    return lax.dot_general(
        left, right, (((1,), (1,)), ((), ())), preferred_element_type=F32
    ).astype(out)


def t_dot(left, right, out=F32):
    return lax.dot_general(
        left, right, (((0,), (0,)), ((), ())), preferred_element_type=F32
    ).astype(out)


def swap_pair(value):
    count = lax.axis_size("dp")
    return lax.ppermute(value, "dp", [(i, i ^ 1) for i in range(count)])


def swap_mirror(value):
    count = lax.axis_size("dp")
    return lax.ppermute(value, "dp", [(i, count - 1 - i) for i in range(count)])


class Steps:
    def __init__(self):
        self.last = ()

    def __call__(self, function, first, *rest):
        result = function(after(first, *self.last) if self.last else first, *rest)
        self.last = tuple(result) if isinstance(result, (tuple, list)) else (result,)
        return result


def add_kernel(left, right, out):
    out[...] = (left[...].astype(F32) + right[...].astype(F32)).astype(out.dtype)


def add(left, right):
    rows, cols = left.shape
    tile = pl.BlockSpec((rows // 2, cols), lambda i: (i, 0))
    return pl.pallas_call(
        add_kernel,
        grid=(2,),
        in_specs=[tile, tile],
        out_specs=tile,
        out_shape=jax.ShapeDtypeStruct((rows, cols), BF16),
        compiler_params=pltpu.CompilerParams(vmem_limit_bytes=SMALL_VMEM_BYTES),
        cost_estimate=lasting(2.2),
        name="add",
    )(left, right)


def split_add_kernel(side, own_a, other_a, own_b, other_b, give, kept):
    give[...] = (own_a[...].astype(F32) + other_a[...].astype(F32)).astype(BF16)
    kept[...] = (own_b[...].astype(F32) + other_b[...].astype(F32)).astype(BF16)


def split_add(side, own, other):
    rows, cols = own.shape
    tile = (rows // 4, cols)
    give = pl.BlockSpec(tile, lambda i, side: ((1 - side[0]) * 2 + i, 0))
    kept = pl.BlockSpec(tile, lambda i, side: (side[0] * 2 + i, 0))
    out = pl.BlockSpec(tile, lambda i, side: (i, 0))
    shape = jax.ShapeDtypeStruct((rows // 2, cols), BF16)
    return pl.pallas_call(
        split_add_kernel,
        grid_spec=pltpu.PrefetchScalarGridSpec(
            num_scalar_prefetch=1,
            grid=(2,),
            in_specs=[give, give, kept, kept],
            out_specs=[out, out],
        ),
        out_shape=[shape, shape],
        compiler_params=pltpu.CompilerParams(vmem_limit_bytes=SMALL_VMEM_BYTES),
        cost_estimate=lasting(2.4),
        name="split_add",
    )(side, own, other, own, other)


def join_kernel(side, total, rest, out):
    is_total = pl.program_id(0) // 2 == side[0]

    @pl.when(is_total)
    def _():
        out[...] = total[...].astype(F32)

    @pl.when(jnp.logical_not(is_total))
    def _():
        out[...] = rest[...].astype(F32)


def join(side, total, rest):
    rows, cols = total.shape
    tile = (rows // 2, cols)
    half = pl.BlockSpec(tile, lambda i, side: (i % 2, 0))
    return pl.pallas_call(
        join_kernel,
        grid_spec=pltpu.PrefetchScalarGridSpec(
            num_scalar_prefetch=1,
            grid=(4,),
            in_specs=[half, half],
            out_specs=pl.BlockSpec(tile, lambda i, side: (i, 0)),
        ),
        out_shape=jax.ShapeDtypeStruct((2 * rows, cols), F32),
        compiler_params=pltpu.CompilerParams(vmem_limit_bytes=SMALL_VMEM_BYTES),
        cost_estimate=lasting(4.0),
        name="join",
    )(side, total, rest)


class DpTotal:
    def __init__(self, steps):
        self.steps = steps
        self.staged = lax.axis_size("dp") == 4
        side = (lax.axis_index("dp") + 1) // 2 % 2
        self.side = jnp.reshape(side, (1,)).astype(jnp.int32)

    def begin(self, own, other):
        if not self.staged:
            self.value = lax.psum(own + other, "dp")
            return
        give, self.keep = self.steps(lambda other: split_add(self.side, own, other), other)
        self.inward = swap_pair(give)

    def middle(self):
        if self.staged:
            self.pair = self.steps(add, self.inward, self.keep)
            self.across = swap_mirror(self.pair)

    def end(self):
        if self.staged:
            self.total = self.steps(add, self.across, self.pair)
            self.rest = swap_pair(self.total)

    def result(self):
        if not self.staged:
            return self.value.astype(F32)
        return self.steps(lambda rest: join(self.side, self.total, rest), self.rest)


def fence_kernel(value, out):
    out[...] = value[...]


class Rounds:
    def __init__(self):
        self.token = jnp.zeros((8, 128), F32)

    def send(self, move, value):
        return move(after(value, self.token))

    def fence(self):
        self.token = pl.pallas_call(
            fence_kernel,
            out_shape=jax.ShapeDtypeStruct((8, 128), F32),
            cost_estimate=HEAVY,
            name="fence",
        )(self.token)

    def wait(self, *results):
        self.fence()
        self.token = after(self.token, *results)


def place_kernel(odd, straight, around, out):
    is_straight = pl.program_id(0) == odd[0]

    @pl.when(is_straight)
    def _():
        out[...] = straight[...]

    @pl.when(jnp.logical_not(is_straight))
    def _():
        out[...] = around[...]


def place_rows(odd, straight, around):
    rows, cols = straight.shape
    whole = pl.BlockSpec((rows, cols), lambda i: (0, 0))
    return pl.pallas_call(
        place_kernel,
        grid=(2,),
        in_specs=[pl.BlockSpec(memory_space=pltpu.SMEM), whole, whole],
        out_specs=pl.BlockSpec((rows, cols), lambda i: (i, 0)),
        out_shape=jax.ShapeDtypeStruct((2 * rows, cols), straight.dtype),
        compiler_params=pltpu.CompilerParams(vmem_limit_bytes=SMALL_VMEM_BYTES),
        cost_estimate=lasting(1.4),
        name="place_rows",
    )(jnp.reshape(odd, (1,)).astype(jnp.int32), straight, around)


def block_bias(first_query, first_key, rows, cols, query_segs, key_segs):
    query_pos = first_query + lax.broadcasted_iota(jnp.int32, (rows, cols), 0)
    key_pos = first_key + lax.broadcasted_iota(jnp.int32, (rows, cols), 1)
    distance = query_pos - key_pos
    allowed = (query_segs == key_segs) & (distance >= 0) & (distance < WINDOW)
    return jnp.where(allowed, 0.0, NEGATIVE)


def first_block(first_query, query_segs, key_segs, tile_k):
    earlier = jnp.sum((key_segs < query_segs[0:1, 0:1]).astype(jnp.int32))
    return lax.div(jnp.maximum(earlier, first_query - (WINDOW - 1)), tile_k)


def attend_forward_kernel(
    start, q_a, q_b, kv, seg_q, seg_k, ctx_a, ctx_b, lse, m_s, l_s, acc_s, *, tq, tk, heads
):
    first_query = start[0] + pl.program_id(0) * tq
    query_segs = seg_q[...]
    low_block = first_block(first_query, query_segs, seg_k[...], tk)
    high_block = lax.div(first_query + tq - 1, tk)
    scale = 1.0 / math.sqrt(HD)

    def step(block, first):
        first_key = pl.multiple_of(block * tk, tk)
        keys = kv[pl.ds(first_key, tk), :HD]
        values = kv[pl.ds(first_key, tk), HD:]
        bias = block_bias(first_query, first_key, tq, tk, query_segs, seg_k[:, pl.ds(first_key, tk)])
        for h in range(2 * heads):
            q = (q_a, q_b)[h // heads]
            own = slice(h % heads * HD, (h % heads + 1) * HD)
            cols = slice(h * HD, (h + 1) * HD)
            scores = dot_t(q[:, own], keys) * scale + bias
            top = jnp.max(scores, axis=1, keepdims=True)
            if first:
                exps = jnp.exp(scores - top)
                l_s[:, cols] = jnp.broadcast_to(jnp.sum(exps, axis=1, keepdims=True), (tq, HD))
                acc_s[:, cols] = dot(exps.astype(BF16), values)
                m_s[:, cols] = jnp.broadcast_to(top, (tq, HD))
            else:
                old = m_s[:, cols]
                new = jnp.maximum(old, top)
                fade = jnp.exp(old - new)
                exps = jnp.exp(scores - jnp.tile(new, (1, tk // HD)))
                l_s[:, cols] = l_s[:, cols] * fade + jnp.sum(exps, axis=1, keepdims=True)
                acc_s[:, cols] = acc_s[:, cols] * fade + dot(exps.astype(BF16), values)
                m_s[:, cols] = new

    step(high_block, True)

    def body(i, _):
        step(high_block - i, False)
        return 0

    lax.fori_loop(1, high_block - low_block + 1, body, 0)
    lane = lax.broadcasted_iota(jnp.int32, (tq, HD), 1)
    logs = jnp.zeros((tq, HD), F32)
    for h in range(2 * heads):
        own = slice(h % heads * HD, (h % heads + 1) * HD)
        cols = slice(h * HD, (h + 1) * HD)
        total = l_s[:, cols]
        (ctx_a, ctx_b)[h // heads][:, own] = (acc_s[:, cols] / total).astype(BF16)
        logs = jnp.where(lane == h, m_s[:, cols] + jnp.log(total), logs)
    lse[...] = logs


def attend_forward(start, q_a, q_b, kv, seg_q, seg_k):
    rows, width = q_a.shape
    tq = tk = 256
    length = kv.shape[0]
    tile = pl.BlockSpec((tq, width), lambda i: (i, 0))
    ctx = jax.ShapeDtypeStruct((rows, width), BF16)
    return pl.pallas_call(
        functools.partial(attend_forward_kernel, tq=tq, tk=tk, heads=width // HD),
        grid=(rows // tq,),
        in_specs=[
            pl.BlockSpec(memory_space=pltpu.SMEM),
            tile,
            tile,
            pl.BlockSpec((length, 2 * HD), lambda i: (0, 0)),
            pl.BlockSpec((tq, 1), lambda i: (i, 0)),
            pl.BlockSpec((1, length), lambda i: (0, 0)),
        ],
        out_specs=[tile, tile, pl.BlockSpec((tq, HD), lambda i: (i, 0))],
        out_shape=[ctx, ctx, jax.ShapeDtypeStruct((rows, HD), F32)],
        scratch_shapes=[pltpu.VMEM((tq, 2 * width), F32)] * 3,
        compiler_params=pltpu.CompilerParams(vmem_limit_bytes=VMEM_BYTES),
        cost_estimate=lasting(8),
        name="attend_forward",
    )(start, q_a, q_b, kv, seg_q, seg_k)


def attend_out_kernel(x, ctx_a, ctx_b, wo_a, wo_b, gain, middle, normed, inverse):
    value = x[...] + dot(ctx_a[...], wo_a[...]) + dot(ctx_b[...], wo_b[...])
    scale = lax.rsqrt(jnp.mean(value * value, axis=1, keepdims=True) + EPSILON)
    middle[...] = value
    normed[...] = (value * scale * gain[...]).astype(BF16)
    inverse[...] = scale


def attend_out(x, ctx_a, ctx_b, wo_a, wo_b, gain):
    rows, width = x.shape
    half = ctx_a.shape[1]
    tm = 256
    tile = pl.BlockSpec((tm, width), lambda i: (i, 0))
    part = pl.BlockSpec((tm, half), lambda i: (i, 0))
    weight = pl.BlockSpec((half, width), lambda i: (0, 0))
    return pl.pallas_call(
        attend_out_kernel,
        grid=(rows // tm,),
        in_specs=[tile, part, part, weight, weight, pl.BlockSpec((1, width), lambda i: (0, 0))],
        out_specs=[tile, tile, pl.BlockSpec((tm, 1), lambda i: (i, 0))],
        out_shape=[
            jax.ShapeDtypeStruct((rows, width), F32),
            jax.ShapeDtypeStruct((rows, width), BF16),
            jax.ShapeDtypeStruct((rows, 1), F32),
        ],
        compiler_params=pltpu.CompilerParams(vmem_limit_bytes=VMEM_BYTES),
        cost_estimate=lasting(5),
        name="attend_out",
    )(x, ctx_a, ctx_b, wo_a, wo_b, gain)


def attend_backward_kernel(
    start, q_a, q_b, kv, seg_q, seg_k, ctx_a, ctx_b, lse, dctx_a, dctx_b, dq_a, dq_b, dkv, dq_s,
    *, tq, tk, heads,
):
    first_query = start[0] + pl.program_id(0) * tq
    query_segs = seg_q[...]
    low_block = first_block(first_query, query_segs, seg_k[...], tk)
    high_block = lax.div(first_query + tq - 1, tk)
    scale = 1.0 / math.sqrt(HD)

    @pl.when(pl.program_id(0) == 0)
    def _():
        dkv[...] = jnp.zeros_like(dkv)

    dq_s[...] = jnp.zeros_like(dq_s)
    logs = lse[...]

    def body(i, _):
        first_key = pl.multiple_of((high_block - i) * tk, tk)
        keys = kv[pl.ds(first_key, tk), :HD]
        values = kv[pl.ds(first_key, tk), HD:]
        bias = block_bias(first_query, first_key, tq, tk, query_segs, seg_k[:, pl.ds(first_key, tk)])
        dk = jnp.zeros((tk, HD), F32)
        dv = jnp.zeros((tk, HD), F32)
        for h in range(2 * heads):
            own = slice(h % heads * HD, (h % heads + 1) * HD)
            cols = slice(h * HD, (h + 1) * HD)
            q_h = (q_a, q_b)[h // heads][:, own]
            do_h = (dctx_a, dctx_b)[h // heads][:, own]
            ctx_h = (ctx_a, ctx_b)[h // heads][:, own]
            inner = jnp.sum(do_h.astype(F32) * ctx_h.astype(F32), axis=1, keepdims=True)
            scores = dot_t(q_h, keys) * scale + bias
            probs = jnp.exp(scores - logs[:, h : h + 1])
            dprobs = dot_t(do_h, values)
            dscores = (probs * (dprobs - inner)).astype(BF16)
            dq_s[:, cols] += dot(dscores, keys)
            dk = dk + t_dot(dscores, q_h)
            dv = dv + t_dot(probs.astype(BF16), do_h)
        dkv[pl.ds(first_key, tk), :HD] += dk * scale
        dkv[pl.ds(first_key, tk), HD:] += dv
        return 0

    lax.fori_loop(0, high_block - low_block + 1, body, 0)
    half = heads * HD
    dq_a[...] = (dq_s[:, :half] * scale).astype(BF16)
    dq_b[...] = (dq_s[:, half:] * scale).astype(BF16)


def attend_backward(start, q_a, q_b, kv, seg_q, seg_k, ctx_a, ctx_b, lse, dctx_a, dctx_b):
    rows, width = q_a.shape
    tq = tk = 256
    length = kv.shape[0]
    tile = pl.BlockSpec((tq, width), lambda i: (i, 0))
    dq = jax.ShapeDtypeStruct((rows, width), BF16)
    return pl.pallas_call(
        functools.partial(attend_backward_kernel, tq=tq, tk=tk, heads=width // HD),
        grid=(rows // tq,),
        in_specs=[
            pl.BlockSpec(memory_space=pltpu.SMEM),
            tile,
            tile,
            pl.BlockSpec((length, 2 * HD), lambda i: (0, 0)),
            pl.BlockSpec((tq, 1), lambda i: (i, 0)),
            pl.BlockSpec((1, length), lambda i: (0, 0)),
            tile,
            tile,
            pl.BlockSpec((tq, HD), lambda i: (i, 0)),
            tile,
            tile,
        ],
        out_specs=[tile, tile, pl.BlockSpec((length, 2 * HD), lambda i: (0, 0))],
        out_shape=[dq, dq, jax.ShapeDtypeStruct((length, 2 * HD), F32)],
        scratch_shapes=[pltpu.VMEM((tq, 2 * width), F32)],
        compiler_params=pltpu.CompilerParams(vmem_limit_bytes=VMEM_BYTES),
        cost_estimate=lasting(20),
        name="attend_backward",
    )(start, q_a, q_b, kv, seg_q, seg_k, ctx_a, ctx_b, lse, dctx_a, dctx_b)


def feed_kernel(
    n2_a, n2_b, dy_a, dy_b, dy_c, dy_d, wg_a, wg_b, wu_a, wu_b, wd_a, wd_b, hidden, dgate, dup, *, tm
):
    root = math.sqrt(2.0 / math.pi)
    rows = n2_a.shape[0]
    feats = wg_a.shape[0]
    for base, n2, first_dy, second_dy in ((0, n2_a, dy_a, dy_b), (rows, n2_b, dy_c, dy_d)):
        for first in range(0, rows, tm):
            own = slice(first, first + tm)
            low, high = n2[own, :feats], n2[own, feats:]
            gate = dot(low, wg_a[...]) + dot(high, wg_b[...])
            up = dot(low, wu_a[...]) + dot(high, wu_b[...])
            dh = dot_t(first_dy[own], wd_a[...]) + dot_t(second_dy[own], wd_b[...])
            square = gate * gate
            tanh = jnp.tanh(gate * (root + (root * 0.044715) * square))
            half = 0.5 + 0.5 * tanh
            act = gate * half
            slope = half + act * (1.0 - tanh) * (root + (3.0 * 0.044715 * root) * square)
            out = slice(base + first, base + first + tm)
            hidden[out] = (act * up).astype(BF16)
            dgate[out] = (dh * up * slope).astype(BF16)
            dup[out] = (dh * act).astype(BF16)


def feed(n2s, dys, wg, wu, wd):
    rows, width = n2s[0].shape
    feats, units = wg[0].shape
    tn = 256
    whole = pl.BlockSpec((rows, width), lambda j: (0, 0))
    half = pl.BlockSpec((rows, feats), lambda j: (0, 0))
    out = jax.ShapeDtypeStruct((2 * rows, units), BF16)
    return pl.pallas_call(
        functools.partial(feed_kernel, tm=min(512, rows)),
        grid=(pl.cdiv(units, tn),),
        in_specs=[whole] * 2
        + [half] * 4
        + [pl.BlockSpec((feats, tn), lambda j: (0, j))] * 4
        + [pl.BlockSpec((tn, feats), lambda j: (j, 0))] * 2,
        out_specs=[pl.BlockSpec((2 * rows, tn), lambda j: (0, j))] * 3,
        out_shape=[out] * 3,
        compiler_params=pltpu.CompilerParams(vmem_limit_bytes=VMEM_BYTES),
        cost_estimate=lasting(17.5),
        name="feed",
    )(*n2s, *dys, *wg, *wu, *wd)


def weight_grad_kernel(*refs):
    out = refs[-1]
    pairs = len(refs) // 2
    total = None
    for left, right in zip(refs[:pairs], refs[pairs:-1]):
        part = t_dot(left[...], right[...])
        total = part if total is None else total + part
    out[...] = total.astype(BF16)


def weight_grad(lefts, rights, name):
    width_left = lefts[0][4]
    width_right = rights[0][4]
    tn = 256

    def left_spec(block):
        _, at, rows, col, cols = block
        return pl.BlockSpec((rows, cols), lambda j: (at, col))

    def right_spec(block):
        _, at, rows, col, cols = block
        return pl.BlockSpec((rows, tn), lambda j: (at, col * (cols // tn) + j))

    out = jax.ShapeDtypeStruct((width_left, width_right), BF16)
    tokens = sum(block[2] for block in lefts)
    return pl.pallas_call(
        weight_grad_kernel,
        grid=(pl.cdiv(width_right, tn),),
        in_specs=[left_spec(b) for b in lefts] + [right_spec(b) for b in rights],
        out_specs=pl.BlockSpec((width_left, tn), lambda j: (0, j)),
        out_shape=out,
        compiler_params=pltpu.CompilerParams(vmem_limit_bytes=MATMUL_VMEM_BYTES),
        cost_estimate=lasting(7.5),
        name=name,
    )(*[b[0] for b in lefts], *[b[0] for b in rights])


def project_kernel(*refs, lefts, multiply):
    left = refs[:lefts]
    weights = refs[lefts : 3 * lefts]
    first, second = refs[3 * lefts :]
    rows = first.shape[0]
    in_first = pl.program_id(0) < pl.num_programs(0) // 2

    def fill(chosen):
        for at, out in ((0, first), (rows, second)):
            own = slice(at, at + rows)
            out[...] = sum(multiply(l[own], w[...]) for l, w in zip(left, chosen)).astype(BF16)

    pl.when(in_first)(lambda: fill(weights[0::2]))
    pl.when(jnp.logical_not(in_first))(lambda: fill(weights[1::2]))


def project(lefts, weights, transposed, name):
    rows, units = lefts[0].shape
    feats = weights[0][0].shape[0 if transposed else 1]
    tn = 256
    tiles = feats // tn
    whole = pl.BlockSpec((rows, units), lambda j: (0, 0))

    def low(j):
        return jnp.minimum(j, tiles - 1)

    def high(j):
        return jnp.maximum(j - tiles, 0)

    if transposed:
        specs = [pl.BlockSpec((tn, units), lambda j, f=f: (f(j), 0)) for f in (low, high)]
    else:
        specs = [pl.BlockSpec((units, tn), lambda j, f=f: (0, f(j))) for f in (low, high)]
    out = jax.ShapeDtypeStruct((rows // 2, 2 * feats), BF16)
    flat = [half for weight in weights for half in weight]
    return pl.pallas_call(
        functools.partial(
            project_kernel, lefts=len(lefts), multiply=dot_t if transposed else dot
        ),
        grid=(2 * tiles,),
        in_specs=[whole] * len(lefts) + specs * len(lefts),
        out_specs=[pl.BlockSpec((rows // 2, tn), lambda j: (0, j))] * 2,
        out_shape=[out] * 2,
        compiler_params=pltpu.CompilerParams(vmem_limit_bytes=MATMUL_VMEM_BYTES),
        cost_estimate=lasting(8.5),
        name=name,
    )(*lefts, *flat)


def per_device(
    tokens_in,
    norm1_gain,
    w_query,
    w_keyval,
    w_attn_out,
    norm2_gain,
    w_gate,
    w_up,
    w_down,
    segment_ids,
    out_cotangent,
):
    width = D
    row = lax.axis_index("row")
    col = lax.axis_index("col")
    local = tokens_in.shape[0]
    mine = local // 2
    feats = tokens_in.shape[1]
    length = segment_ids.shape[1]
    spans = length // local

    def keep(value):
        return lax.dynamic_slice_in_dim(value, row * mine, mine, 0)

    def give(value):
        return lax.dynamic_slice_in_dim(value, (1 - row) * mine, mine, 0)

    is_low = row == 0

    odd = lax.axis_index("dp") % 2
    paired = lax.axis_size("dp") % 2 == 0

    def straight_part(weight):
        span = weight.shape[0] // 2
        return lax.dynamic_slice_in_dim(weight, odd * span, span, 0) if paired else weight

    def placed(straight, around):
        return place_rows(odd, straight, around) if paired else straight

    def send_pair(straight):
        return rounds.send(swap_pair, straight) if paired else straight

    rounds = Rounds()
    small = jnp.concatenate([norm1_gain, norm2_gain, segment_ids.reshape(-1).astype(F32)])
    heads_own = w_query.shape[1]
    small_in = rounds.send(swap_row, small)
    x_in = rounds.send(swap_row, give(tokens_in))
    dy_own = keep(out_cotangent)
    dy_far_own = rounds.send(swap_far, dy_own)
    wq_far_own = swap_far(after(w_query, dy_own))
    w_qkv = jnp.concatenate([w_query, w_keyval], axis=1)
    wqkv_in = swap_row(after(w_qkv, small_in))
    rounds.wait(x_in, dy_far_own, small_in)

    wo_far_own = rounds.send(swap_far, w_attn_out)
    wo_in = rounds.send(swap_row, w_attn_out)
    gain_one = jnp.concatenate([norm1_gain, small_in[:feats]])
    gain_two = jnp.concatenate([norm2_gain, small_in[feats : 2 * feats]])
    segs_in = small_in[2 * feats :].astype(jnp.int32).reshape(segment_ids.shape)
    segs_all = jnp.concatenate(
        [jnp.where(is_low, segment_ids, segs_in), jnp.where(is_low, segs_in, segment_ids)], axis=0
    )
    x = jnp.concatenate([keep(tokens_in), x_in], axis=1).astype(F32)
    inverse_one = lax.rsqrt(jnp.mean(x * x, axis=1, keepdims=True) + EPSILON)
    normed_one = (x * inverse_one * gain_one).astype(BF16)
    place = col % spans
    seg_row = lax.dynamic_slice_in_dim(segs_all, col // spans, 1, 0)
    first_token = place * local + row * mine
    seg_q = lax.dynamic_slice_in_dim(seg_row[0], first_token, mine, 0)[:, None]
    start = jnp.reshape(first_token, (1,)).astype(jnp.int32)
    rounds.wait(wqkv_in, wq_far_own, normed_one)

    wq_in = wqkv_in[:, :heads_own]
    wq_far_in = rounds.send(swap_far, wq_in)
    wkv = jnp.concatenate([w_keyval, wqkv_in[:, heads_own:]], axis=0)
    kv_own = dot(normed_one, wkv, BF16)
    rounds.wait(kv_own)
    kv_in = rounds.send(swap_row, kv_own)
    rounds.fence()
    wg_straight = rounds.send(swap_row, straight_part(w_gate))
    rounds.wait(wo_in, kv_in, wq_far_in, wo_far_own)

    kv_pair = jnp.concatenate(
        [jnp.where(is_low, kv_own, kv_in), jnp.where(is_low, kv_in, kv_own)], axis=0
    )
    wq_half = jnp.concatenate(
        [
            jnp.concatenate([w_query, wq_far_own], axis=1),
            jnp.concatenate([wq_in, wq_far_in], axis=1),
        ],
        axis=0,
    )
    wo_far_in = rounds.send(swap_far, wo_in)
    wu_straight = rounds.send(swap_row, straight_part(w_up))
    wq_core = rounds.send(swap_core, wq_half)
    if spans == 2:
        kv_far = rounds.send(swap_core, kv_pair)
        first = place == 0
        kv = jnp.concatenate(
            [jnp.where(first, kv_pair, kv_far), jnp.where(first, kv_far, kv_pair)], axis=0
        )
    else:
        kv = kv_pair
    q_a = dot(normed_one, wq_half, BF16)
    rounds.wait(kv, wq_core, q_a)

    q_b = dot(normed_one, wq_core, BF16)
    ctx_a, ctx_b, lse = attend_forward(start, after(q_a, rounds.token), q_b, kv, seg_q, seg_row)
    rounds.wait(wo_far_in, wg_straight, ctx_a)

    wo_half = jnp.concatenate(
        [
            jnp.concatenate([w_attn_out, wo_far_own], axis=0),
            jnp.concatenate([wo_in, after(wo_far_in, rounds.token)], axis=0),
        ],
        axis=1,
    )
    wo_core = rounds.send(swap_core, wo_half)
    wg_around = send_pair(wg_straight)
    wd_straight = rounds.send(swap_row, straight_part(w_down))
    middle, n2, inverse_two = attend_out(
        x, after(ctx_a, rounds.token), ctx_b, wo_half, wo_core, gain_two[None, :]
    )
    rounds.wait(n2, wo_core)

    n2_far = rounds.send(swap_far, n2)
    n2_near = rounds.send(swap_core, n2)
    rounds.wait(n2_near, wu_straight, wg_around)

    dy_in = rounds.send(swap_row, give(out_cotangent))
    wu_around = send_pair(wu_straight)
    dy_near_own = rounds.send(swap_core, dy_own)
    rounds.wait(wd_straight, wu_around, dy_near_own)

    wd_around = send_pair(wd_straight)
    dy_diagonal_own = rounds.send(swap_core, dy_far_own)
    wg = (w_gate, placed(wg_straight, after(wg_around, rounds.token)))
    wu = (w_up, placed(wu_straight, after(wu_around, wg[1])))
    rounds.wait(dy_in, n2_far, dy_diagonal_own)

    dy_far_in = rounds.send(swap_far, dy_in)
    dy_near_in = rounds.send(swap_core, dy_in)
    n2_diagonal = rounds.send(swap_core, n2_far)
    wd = (w_down, placed(wd_straight, after(wd_around, rounds.token)))
    dy_near = (dy_near_own, dy_near_in)
    hidden_a, dgate_a, dup_a = feed((n2, n2_near), (dy_own, dy_in, *dy_near), wg, wu, wd)
    dy_diagonal = (dy_diagonal_own, swap_core(dy_far_in))
    hidden_b, dgate_b, dup_b = feed(
        (after(n2_far, hidden_a), n2_diagonal), (dy_far_own, dy_far_in, *dy_diagonal), wg, wu, wd
    )

    normed = [n2, n2_near, n2_far, n2_diagonal]
    cotangents = [(dy_own, dy_in), dy_near, (dy_far_own, dy_far_in), dy_diagonal]
    units = w_gate.shape[1]

    def normed_blocks(half):
        return [(value, 0, mine, half, feats) for value in normed]

    def cotangent_blocks(half):
        return [(value[half], 0, mine, 0, feats) for value in cotangents]

    def unit_blocks(first_pair, second_pair, *earlier):
        if earlier:
            first_pair = after(first_pair, *earlier)
        return [
            (value, at, mine, 0, units) for value in (first_pair, second_pair) for at in range(2)
        ]

    steps = Steps()

    def gate_grad(half):
        return steps(
            lambda last: weight_grad(normed_blocks(half), unit_blocks(dgate_a, last), "w_gate_grad"),
            dgate_b,
        )

    def up_grad(half):
        return steps(
            lambda last: weight_grad(normed_blocks(half), unit_blocks(dup_a, last), "w_up_grad"),
            dup_b,
        )

    def down_grad(half):
        return steps(
            lambda last: weight_grad(
                unit_blocks(hidden_a, last), cotangent_blocks(half), "w_down_grad"
            ),
            hidden_b,
        )

    gate_sum, up_sum, down_sum, rest_sum = [DpTotal(steps) for _ in range(4)]
    gate_in = swap_row(gate_grad(1))
    dn2_far, dn2_diagonal = steps(
        lambda dgate: project([dgate, dup_b], [wg, wu], True, "feed_back"), dgate_b
    )
    diagonal_in = swap_core(dn2_diagonal)
    gate_own = gate_grad(0)
    for_far = steps(
        lambda into: (dn2_far.astype(F32) + into.astype(F32)).astype(BF16), diagonal_in
    )
    far_in = swap_far(for_far)
    up_in = swap_row(up_grad(1))
    dn2_own, dn2_near = steps(
        lambda dgate: project([dgate, dup_a], [wg, wu], True, "feed_back"), dgate_a
    )
    near_in = swap_core(dn2_near)
    gate_sum.begin(gate_own, gate_in)
    up_own = up_grad(0)

    def middle_back(far):
        dnormed = dn2_own.astype(F32) + near_in.astype(F32) + far.astype(F32)
        scaled = dnormed * gain_two
        projection = jnp.mean(scaled * middle, axis=1, keepdims=True)
        dmiddle = (
            jnp.concatenate([dy_own, dy_in], axis=1).astype(F32)
            + inverse_two * scaled
            - middle * (inverse_two**3 * projection)
        )
        return dmiddle, dmiddle.astype(BF16), jnp.sum(dnormed * middle * inverse_two, axis=0)

    dmiddle, dattn, gain_two_part = steps(middle_back, far_in)
    gate_sum.middle()
    down_in = swap_row(down_grad(1))

    dctx_a, dctx_b = steps(lambda d: (dot_t(d, wo_half, BF16), dot_t(d, wo_core, BF16)), dattn)
    up_sum.begin(up_own, up_in)
    out_core = swap_core(steps(lambda d: t_dot(d, ctx_b, BF16), dattn))
    down_own = down_grad(0)
    out_part = steps(lambda d: t_dot(d, ctx_a, BF16), dattn)
    out_chip = steps(add, out_core, out_part)
    out_far = swap_far(out_chip[:, heads_own:])
    dq_a, dq_b, dkv_all = steps(
        lambda d: attend_backward(
            start, q_a, q_b, kv, seg_q, seg_row, ctx_a, ctx_b, lse, d, dctx_b
        ),
        dctx_a,
    )
    if spans == 2:
        is_first = place == 0

        def other_half(value):
            return jnp.where(is_first, value[local:], value[:local]).astype(BF16)

        dkv_core = swap_core(steps(other_half, dkv_all))
    up_sum.middle()
    gate_sum.end()
    out_mine = steps(add, out_far, out_chip[:, :heads_own])
    out_row = swap_row(out_mine[feats:])
    down_sum.begin(down_own, down_in)
    query_core = swap_core(steps(lambda d: t_dot(normed_one, d, BF16), dq_b))
    query_part = steps(lambda d: t_dot(normed_one, d, BF16), dq_a)
    ffn_far, ffn_diagonal = steps(lambda h: project([h], [wd], False, "down"), hidden_b)
    query_chip = steps(add, query_core, query_part)
    query_far = swap_far(query_chip[:, heads_own:])
    if spans == 2:

        def pair_of(core):
            value = jnp.where(is_first, dkv_all[:local], dkv_all[local:]) + core.astype(F32)
            return keep(value), give(value).astype(BF16)

        dkv_keep, dkv_give = steps(pair_of, dkv_core)
    else:
        dkv_keep, dkv_give = keep(dkv_all), give(dkv_all).astype(BF16)
    dkv_row = swap_row(dkv_give)
    gate_total = gate_sum.result()
    dkv = steps(lambda other: (dkv_keep + other.astype(F32)).astype(BF16), dkv_row)

    def norm_one_back(dkv):
        dnormed = dot_t(dq_a, wq_half) + dot_t(dq_b, wq_core) + dot_t(dkv, wkv)
        scaled = dnormed * gain_one
        projection = jnp.mean(scaled * x, axis=1, keepdims=True)
        dx = dmiddle + inverse_one * scaled - x * (inverse_one**3 * projection)
        gain_parts = jnp.stack([jnp.sum(dnormed * x * inverse_one, axis=0), gain_two_part], axis=1)
        kv_part = t_dot(normed_one, dkv, BF16)
        small_part = jnp.pad(gain_parts, ((0, 0), (0, HD - 2))).astype(BF16)
        return dx, dx[:, feats:].astype(BF16), jnp.concatenate([kv_part, small_part], axis=1)

    dx, dx_give, small_part = steps(norm_one_back, dkv)
    small_row = swap_row(small_part[feats:])
    ffn_diagonal_in = swap_core(after(ffn_diagonal, small_part))
    up_sum.end()
    down_sum.middle()
    ffn_own, ffn_near = steps(lambda h: project([h], [wd], False, "down"), hidden_a)
    query_mine = steps(add, query_far, query_chip[:, :heads_own])
    query_row = swap_row(query_mine[feats:])
    small_one = steps(add, small_row, small_part[:feats])
    small_core = swap_core(small_one)
    ffn_for_far = steps(add, ffn_diagonal_in, ffn_far)
    small_two = steps(add, small_core, small_one)
    small_far = swap_far(small_two)
    ffn_far_in = swap_far(after(ffn_for_far, small_two))
    ffn_near_in = swap_core(after(ffn_near, small_two))
    up_total = up_sum.result()
    down_sum.end()
    rest_own = jnp.concatenate([out_mine[:feats], query_mine[:feats], small_two], axis=1)
    rest_in = jnp.concatenate([out_row, query_row, small_far], axis=1)
    rest_sum.begin(rest_own, rest_in)
    ffn_chip = steps(add, ffn_near_in, ffn_own)
    rest_sum.middle()

    def add_up(far):
        y = middle + ffn_chip.astype(F32) + far.astype(F32)
        return y, y[:, feats:].astype(BF16)

    y, y_give = steps(add_up, ffn_far_in)
    y_in = swap_row(y_give)
    down_total = down_sum.result()
    dx_in = swap_row(after(dx_give, down_total))
    rest_sum.end()

    def put_back(other, value):
        other = other.astype(F32)
        own = value[:, :feats]
        return jnp.concatenate(
            [jnp.where(is_low, own, other), jnp.where(is_low, other, own)], axis=0
        )

    dx_out = steps(put_back, dx_in, dx)
    y_out = steps(put_back, y_in, y)
    rest_total = rest_sum.result()
    out_total = rest_total[:, :heads_own].T
    query_total = rest_total[:, heads_own : 2 * heads_own]
    kv_total = rest_total[:, 2 * heads_own : 2 * heads_own + 2 * HD]
    gain_total = rest_total[:, 2 * heads_own + 2 * HD : 2 * heads_own + 2 * HD + 2].T

    return (
        y_out,
        dx_out,
        query_total,
        kv_total,
        out_total,
        gate_total,
        up_total,
        down_total,
        gain_total[0],
        gain_total[1],
    )


def solution(mesh):
    return jax.shard_map(
        per_device,
        mesh=mesh,
        in_specs=(
            P(("dp", "col"), "row"),
            P("row"),
            P("row", "col"),
            P("row", None),
            P("col", "row"),
            P("row"),
            P("row", "col"),
            P("row", "col"),
            P("col", "row"),
            P(("dp", "row"), None),
            P(("dp", "col"), "row"),
        ),
        out_specs=(
            P(("dp", "col"), "row"),
            P(("dp", "col"), "row"),
            P("row", "col"),
            P("row", None),
            P("col", "row"),
            P("row", "col"),
            P("row", "col"),
            P("col", "row"),
            P("row"),
            P("row"),
        ),
        check_vma=False,
    )
```
